256 devices in a mesh: dp: 16 (over y, x), shard: 16 (over z, core).
Axes of the slice: x: 4, y: 4, z: 8, core: 2. Of those that a mesh axis runs over, the one named last changes fastest.
Arguments:
- grad_partial: bfloat16 [16, 16, 1024, 1024], P('dp', None, 'shard'), may hold values from -64 to 64
- owner_slots: int32 [16], replicated, may hold values from 0 to 15, each once
- left_roots: float32 [16, 1024, 1024], P('shard', None, 'dp'), may hold values from -0.2 to 1.6, as said below
- right_roots: float32 [16, 1024, 1024], P('shard', 'dp'), may hold values from -0.2 to 1.6, as said below
- momentum: float32 [16, 1024, 1024], P('shard', 'dp'), may hold values from -6 to 6
Outputs:
- direction: bfloat16 [16, 1024, 1024], P(None, ('dp', 'shard'))
- new_momentum: float32 [16, 1024, 1024], P('shard', 'dp')
The draws below stay inside these ranges and needn't reach their ends.
Inputs may be any that keep to these rules, and one draw needn't show every extreme that they name: `owner_slots`: every slot is named once; slot p is owned by shard index p. `left_roots`: every block is symmetric. `right_roots`: every block is symmetric.
All inputs are finite; a program needn't handle non-finite values.
Results may differ from the reference program's by a relative error of at most 0.0006.
Values may be sent and summed in bfloat16 or wider, within the bound.
A program may use at most 64 MiB of HBM per device.

```python
import math
import jax
import jax.numpy as jnp
from jax import lax

BS = 1024
NBLK = 16
N_DP = 16


def symmetric_blocks(off_part, diag_part):
    mirrored = 0.5 * (off_part + jnp.swapaxes(off_part, 1, 2))
    return mirrored + jnp.eye(BS, dtype=jnp.float32)[None, :, :] * diag_part[:, :, None]


def draw_grad_partial(key, part):
    key = jax.random.fold_in(key, 11)
    key_noise, key_rows, key_cols = jax.random.split(key, 3)
    row_scale = jnp.exp(jax.random.uniform(key_rows, (1, NBLK, BS, 1), jnp.float32) * math.log(10.0))
    col_scale = jnp.exp(jax.random.uniform(key_cols, (1, NBLK, 1, BS), jnp.float32) * math.log(10.0))
    position = jnp.arange(BS, dtype=jnp.float32) / BS
    noise = jnp.clip(jax.random.normal(key_noise, (N_DP, NBLK, BS, BS), jnp.float32), -5.0, 5.0)
    rising = jnp.exp(position * math.log(3.0))
    values = noise * rising[None, None, :, None] * row_scale * col_scale / 40.0
    return values.astype(jnp.bfloat16)


def draw_left_roots(key, part):
    key = jax.random.fold_in(key, 21)
    key_off, key_diag = jax.random.split(key)
    off_part = 0.02 * jnp.clip(jax.random.normal(key_off, (NBLK, BS, BS), jnp.float32), -4.0, 4.0)
    diag_part = jax.random.uniform(key_diag, (NBLK, BS), jnp.float32, 0.6, 1.4)
    return symmetric_blocks(off_part, diag_part)


def draw_right_roots(key, part):
    key = jax.random.fold_in(key, 31)
    key_off, key_diag = jax.random.split(key)
    off_part = 0.02 * jnp.clip(jax.random.normal(key_off, (NBLK, BS, BS), jnp.float32), -4.0, 4.0)
    diag_part = jax.random.uniform(key_diag, (NBLK, BS), jnp.float32, 0.6, 1.4)
    return symmetric_blocks(off_part, diag_part)


def levels(stream_key, shape, cuts, smallest, top_value):
    loudness, own = 1.0, jax.random.fold_in(stream_key, 6)
    for axis_at, blocks in cuts:
        steps = jnp.exp(jax.random.uniform(jax.random.fold_in(own, axis_at), (blocks,), jnp.float32, smallest / len(cuts), top_value / len(cuts)))
        loudness = loudness * jnp.repeat(steps, shape[axis_at] // blocks).reshape([-1 if axis == axis_at else 1 for axis in range(len(shape))])
    return loudness


def normal_values(rng, dims, scale, most, pieces=(), held_as=jnp.bfloat16):
    array = scale * jax.random.normal(rng, dims, jnp.float32)
    if pieces:
        array = array * levels(rng, dims, pieces, -0.22, 0.18)
    return jnp.clip(array, -most, most).astype(held_as)


def setup_inputs(seed: int = 0) -> dict:
    seeds = jax.random.split(jax.random.key(seed), 6)
    grad_partial = draw_grad_partial(jax.random.fold_in(seeds[5], 71), 0)
    owner_slots = jax.random.permutation(seeds[1], NBLK).astype(jnp.int32)
    left_roots = draw_left_roots(jax.random.fold_in(seeds[5], 71), 0)
    right_roots = draw_right_roots(jax.random.fold_in(seeds[5], 71), 0)
    momentum = normal_values(seeds[4], (NBLK, BS, BS), 1.0, 6.0, ((0, 16), (1, 16)), jnp.float32)
    return {"grad_partial": grad_partial, "owner_slots": owner_slots, "left_roots": left_roots, "right_roots": right_roots, "momentum": momentum}


epsilon = 1e-06
decay_rate = 0.9

def reference(grad_partial, owner_slots, left_roots, right_roots, momentum):
    counting = jnp.arange(NBLK, dtype=jnp.int32)
    inverse = jnp.zeros((NBLK,), jnp.int32).at[owner_slots].set(counting)

    def per_slot(slot):
        block = inverse[slot]
        gradient = lax.optimization_barrier(jnp.sum(grad_partial[:, block].astype(jnp.float32), axis=0))
        right_part = jnp.dot(gradient, right_roots[slot], precision=lax.Precision.HIGHEST, preferred_element_type=jnp.float32)
        precond = jnp.dot(left_roots[slot], right_part, precision=lax.Precision.HIGHEST, preferred_element_type=jnp.float32)
        grad_sq = jnp.sum(gradient * gradient)
        prec_sq = jnp.sum(precond * precond)
        entries = BS * BS
        graft_scale = jnp.sqrt(grad_sq / entries + epsilon) / jnp.sqrt(prec_sq / entries + epsilon)
        graft = precond * graft_scale
        moved = decay_rate * momentum[slot] + graft
        heading = (decay_rate * moved + graft).astype(jnp.bfloat16)
        return (heading, moved)
    direction_slots, new_momentum = lax.map(per_slot, counting)
    return (jnp.take(direction_slots, owner_slots, axis=0), new_momentum)
```

```python
import jax
import jax.numpy as jnp
from jax import lax
from jax.experimental import pallas as pl
from jax.experimental.pallas import tpu as pltpu
from jax.sharding import PartitionSpec as P

epsilon = 1e-06
decay_rate = 0.9

MESH = pl.DeviceIdType.MESH
BF = jnp.bfloat16
F32 = jnp.float32
CHUNKS = 4
OFFSETS = (4, 3, 5, 2, 6, 1, 7, 0)
NT = (((1,), (1,)), ((), ()))
NN = (((1,), (0,)), ((), ()))


def split(value):
    high = value.astype(BF)
    return high, (value - high.astype(F32)).astype(BF)


def dot(a, b, dims):
    return lax.dot_general(a, b, dims, preferred_element_type=F32)


def fold(value):
    rows = value.reshape(32, 8, 256).sum(axis=0)
    return rows[:, :128] + rows[:, 128:]


def kernel(
    gp, own, lr, rr, mo, dir_o, nm_o,
    gv, lv, rv, mv, stx, sty, r1x, r1y, s1x, s1y, r2x, r2y, zt, buf_y, buf_x, lg, rg,
    pt, pr, scx, scy, h32, hb, fin, ob, nm,
    loc, s1s, s1r, s2s, s2r, zs, zr, ls, lrc, rs, rrc, gys, gyr, gxs, gxr, ts, tr,
    cxs, cxr, cys, cyr, fs, fr,
):
    dp = lax.axis_index("dp")
    shard = lax.axis_index("shard")
    x, y = lax.rem(dp, 4), lax.div(dp, 4)
    z, core = lax.div(shard, 2), lax.rem(shard, 2)

    def xp(k):
        return lax.rem(x + k, 4)

    def yp(k):
        return lax.rem(y + k, 4)

    def to_x(k):
        return {"dp": y * 4 + xp(k)}

    def to_y(k):
        return {"dp": yp(k) * 4 + x}

    def remote(src, dst, ssem, rsem, device):
        return pltpu.make_async_remote_copy(
            src_ref=src, dst_ref=dst, send_sem=ssem, recv_sem=rsem, device_id=device, device_id_type=MESH
        )

    load_g = pltpu.make_async_copy(gp.at[0], gv, loc.at[0])
    load_l = pltpu.make_async_copy(lr.at[0], lv, loc.at[1])
    load_r = pltpu.make_async_copy(rr.at[0], rv, loc.at[2])
    load_m = pltpu.make_async_copy(mo.at[0], mv, loc.at[3])
    load_g.start()
    load_l.start()
    load_r.start()
    load_m.start()

    barrier = pltpu.get_barrier_semaphore()
    for k in range(1, 4):
        pl.semaphore_signal(barrier, inc=1, device_id=to_x(k), device_id_type=MESH)
        pl.semaphore_signal(barrier, inc=1, device_id=to_y(k), device_id_type=MESH)
    for k in range(1, 16):
        pl.semaphore_signal(
            barrier, inc=1, device_id={"shard": lax.rem(shard + k, 16)}, device_id_type=MESH
        )

    def block_of(slot):
        found = jnp.int32(0)
        for b in range(16):
            found = jnp.where(own[b] == slot, b, found)
        return found

    def stage(q):
        zq = lax.rem(z + OFFSETS[q], 8)
        first = gv[block_of(zq * 2)]
        for i in range(4):
            stx[i, q] = first[16 * i : 16 * i + 16]
        second = gv[block_of(zq * 2 + 1)]
        for j in range(4):
            sty[j, q] = second[:, 256 * j : 256 * j + 256]

    def stage1(c):
        part = pl.ds(2 * c, 2)
        out = []
        for k in range(1, 4):
            out.append(remote(stx.at[xp(k), part], r1x.at[k - 1, part], s1s.at[k - 1, c, 0], s1r.at[k - 1, c, 0], to_x(k)))
            out.append(remote(sty.at[yp(k), part], r1y.at[k - 1, part], s1s.at[k - 1, c, 1], s1r.at[k - 1, c, 1], to_y(k)))
        return out

    def stage2(c):
        part = pl.ds(2 * c, 2)
        out = []
        for k in range(1, 4):
            out.append(remote(s1x.at[yp(k), part], r2x.at[k - 1, part], s2s.at[k - 1, c, 0], s2r.at[k - 1, c, 0], to_y(k)))
            out.append(remote(s1y.at[xp(k), part], r2y.at[k - 1, part], s2s.at[k - 1, c, 1], s2r.at[k - 1, c, 1], to_x(k)))
        return out

    def start_all(copies):
        for copy in copies:
            copy.start()

    def recv_all(copies):
        for copy in copies:
            copy.wait_recv()

    def send_all(copies):
        for copy in copies:
            copy.wait_send()

    def sum1(q):
        total = stx[x, q].astype(F32)
        for k in range(3):
            total = total + r1x[k, q].astype(F32)
        for j in range(4):
            s1x[j, q] = total[:, 256 * j : 256 * j + 256]
        total = sty[y, q].astype(F32)
        for k in range(3):
            total = total + r1y[k, q].astype(F32)
        for i in range(4):
            s1y[i, q] = total[16 * i : 16 * i + 16]

    def sum2(q):
        total = s1x[y, q]
        for k in range(3):
            total = total + r2x[k, q]
        zt[0, q, 0], zt[0, q, 1] = split(total)
        total = s1y[x, q]
        for k in range(3):
            total = total + r2y[k, q]
        zt[1, q, 0], zt[1, q, 1] = split(total)

    def exchange(q, target):
        dst = buf_y.at[y, :, shard] if target == 0 else buf_x.at[:, shard, x]
        device = {"shard": lax.rem(z + OFFSETS[q], 8) * 2 + target}
        return remote(zt.at[target, q], dst, zs.at[target, q], zr.at[q, core], device)

    load_g.wait()
    stage(0)
    stage(1)
    pl.semaphore_wait(barrier, 21)
    start_all(stage1(0))
    for c in range(1, CHUNKS):
        stage(2 * c)
        stage(2 * c + 1)
        start_all(stage1(c))

    def finish2(c):
        recv_all(stage2(c))
        sum2(2 * c)
        sum2(2 * c + 1)
        for q in (2 * c, 2 * c + 1):
            if OFFSETS[q]:
                exchange(q, 0).start()
                exchange(q, 1).start()
            else:
                @pl.when(core == 0)
                def _():
                    exchange(q, 1).start()
                    buf_y[y, :, shard] = zt[0, q]

                @pl.when(core == 1)
                def _():
                    exchange(q, 0).start()
                    buf_x[:, shard, x] = zt[1, q]

    load_l.wait()
    load_r.wait()
    left = split(lv[...])
    right = split(rv[...])
    for h in range(2):
        lg[y, h] = left[h]
        rg[x, h] = right[h]
    roots = []
    for k in range(1, 4):
        roots.append(remote(lg.at[y], lg.at[y], ls.at[k - 1], lrc.at[k - 1], to_y(k)))
        roots.append(remote(rg.at[x], rg.at[x], rs.at[k - 1], rrc.at[k - 1], to_x(k)))

    for c in range(CHUNKS):
        recv_all(stage1(c))
        sum1(2 * c)
        sum1(2 * c + 1)
        start_all(stage2(c))
        if c:
            finish2(c - 1)
    start_all(roots)
    finish2(CHUNKS - 1)

    for c in range(CHUNKS):
        send_all(stage1(c))
        send_all(stage2(c))

    def received(q, source):
        @pl.when(core == 0)
        def _():
            remote(zt.at[0, q], buf_y.at[y, :, shard], zs.at[0, q], zr.at[q, source], {"shard": shard}).wait_recv()

        @pl.when(core == 1)
        def _():
            remote(zt.at[1, q], buf_x.at[:, shard, x], zs.at[1, q], zr.at[q, source], {"shard": shard}).wait_recv()

    for q in range(8):
        if OFFSETS[q]:
            received(q, 0)
            received(q, 1)
        else:
            received(q, 1 - core)

    def gather_y():
        return [remote(buf_y.at[y], buf_y.at[y], gys.at[k - 1], gyr.at[k - 1], to_y(k)) for k in range(1, 4)]

    def gather_x():
        return [
            remote(buf_x.at[:, :, x], buf_x.at[:, :, x], gxs.at[k - 1], gxr.at[k - 1], to_x(k)) for k in range(1, 4)
        ]

    def times_right():
        total = None
        for j in range(4):
            cols = slice(256 * j, 256 * j + 256)
            a_high = buf_y[j, 0].reshape(256, 256)
            a_low = buf_y[j, 1].reshape(256, 256)
            b_high = rg[:, 0, :, cols].reshape(256, 256)
            b_low = rg[:, 1, :, cols].reshape(256, 256)
            part = dot(a_high, b_high, NT) + dot(a_high, b_low, NT) + dot(a_low, b_high, NT)
            total = part if total is None else total + part
        return total

    def left_times():
        a_high = lg[:, 0].reshape(256, 1024)
        a_low = lg[:, 1].reshape(256, 1024)
        b_high = buf_x[0].reshape(1024, 256)
        b_low = buf_x[1].reshape(1024, 256)
        return dot(a_high, b_high, NN) + dot(a_high, b_low, NN) + dot(a_low, b_high, NN)

    lefts, rights = roots[0::2], roots[1::2]

    def finish(tile):
        scx[x, 1] = fold(tile * tile)
        for j in range(4):
            pt[j] = tile[64 * j : 64 * j + 64]

    @pl.when(core == 0)
    def _():
        start_all(gather_y())
        own_tile = (buf_y[y, 0].astype(F32) + buf_y[y, 1].astype(F32)).reshape(256, 256)
        scx[x, 0] = fold(own_tile * own_tile)
        recv_all(rights)
        recv_all(gather_y())
        high, low = split(times_right())
        buf_x[0, :, x] = high.reshape(16, 16, 256)
        buf_x[1, :, x] = low.reshape(16, 16, 256)
        start_all(gather_x())
        recv_all(lefts)
        recv_all(gather_x())
        finish(left_times())

    @pl.when(core == 1)
    def _():
        start_all(gather_x())
        own_tile = (buf_x[0, :, x].astype(F32) + buf_x[1, :, x].astype(F32)).reshape(256, 256)
        scx[x, 0] = fold(own_tile * own_tile)
        recv_all(lefts)
        recv_all(gather_x())
        high, low = split(left_times())
        buf_y[y, 0] = high.reshape(16, 16, 256)
        buf_y[y, 1] = low.reshape(16, 16, 256)
        start_all(gather_y())
        recv_all(rights)
        recv_all(gather_y())
        finish(times_right())

    norms_x = [remote(scx.at[x], scx.at[x], cxs.at[k - 1], cxr.at[k - 1], to_x(k)) for k in range(1, 4)]
    norms_y = [remote(scy.at[y], scy.at[y], cys.at[k - 1], cyr.at[k - 1], to_y(k)) for k in range(1, 4)]
    turn = [remote(pt.at[yp(k)], pr.at[y], ts.at[k - 1], tr.at[k - 1], to_y(k)) for k in range(1, 4)]
    start_all(norms_x)
    start_all(turn)
    pr[y] = pt[y]
    load_m.wait()
    send_all(gather_x())
    send_all(gather_y())
    send_all(roots)
    recv_all(norms_x)
    scy[y] = scx[0] + scx[1] + scx[2] + scx[3]
    start_all(norms_y)
    recv_all(turn)
    recv_all(norms_y)
    sums = scy[0] + scy[1] + scy[2] + scy[3]
    entries = 1024 * 1024
    grad_total = jnp.sum(sums[0], keepdims=True)
    prec_total = jnp.sum(sums[1], keepdims=True)
    scale = jnp.sqrt(grad_total / entries + epsilon) / jnp.sqrt(prec_total / entries + epsilon)
    for j in range(4):
        cols = slice(256 * j, 256 * j + 256)
        graft = pr[j] * scale
        moved = decay_rate * mv[:, cols] + graft
        nm[:, cols] = moved
        heading = decay_rate * moved + graft
        h32[pl.ds(2 * j, 64, stride=8), :] = heading[:, :128]
        h32[pl.ds(2 * j + 1, 64, stride=8), :] = heading[:, 128:]
    hb[...] = h32[...].reshape(16, 32, 128).astype(BF)

    def back(k):
        to = lax.rem(shard + k, 16)
        return remote(hb.at[to], fin.at[shard], fs.at[k], fr.at[k], {"shard": to})

    order = (8, 9, 7, 10, 6, 11, 5, 12, 4, 13, 3, 14, 2, 15, 1)
    for k in order:
        back(k).start()
    store_m = pltpu.make_async_copy(nm, nm_o.at[0], loc.at[4])
    store_m.start()
    fin[shard] = hb[shard]
    send_all(norms_x)
    send_all(norms_y)
    send_all(turn)
    for q in range(8):
        if OFFSETS[q]:
            exchange(q, 0).wait_send()
            exchange(q, 1).wait_send()
        else:
            @pl.when(core == 0)
            def _():
                exchange(q, 1).wait_send()

            @pl.when(core == 1)
            def _():
                exchange(q, 0).wait_send()

    for k in order:
        back(k).wait_recv()
    for b in range(16):
        ob[b] = fin[own[b]]
    store_d = pltpu.make_async_copy(ob, dir_o, loc.at[5])
    store_d.start()
    for k in order:
        back(k).wait_send()
    store_m.wait()
    store_d.wait()


def body(grad_partial, owner_slots, left_roots, right_roots, momentum):
    dma = pltpu.SemaphoreType.DMA
    any_space = pl.BlockSpec(memory_space=pl.ANY)
    direction, new_momentum = pl.pallas_call(
        kernel,
        out_shape=(
            jax.ShapeDtypeStruct((16, 32, 128), BF),
            jax.ShapeDtypeStruct((1, 64, 1024), F32),
        ),
        in_specs=[any_space, pl.BlockSpec(memory_space=pltpu.SMEM), any_space, any_space, any_space],
        out_specs=(any_space, any_space),
        scratch_shapes=[
            pltpu.VMEM((16, 64, 1024), BF),
            pltpu.VMEM((64, 1024), F32),
            pltpu.VMEM((64, 1024), F32),
            pltpu.VMEM((64, 1024), F32),
            pltpu.VMEM((4, 8, 16, 1024), BF),
            pltpu.VMEM((4, 8, 64, 256), BF),
            pltpu.VMEM((3, 8, 16, 1024), BF),
            pltpu.VMEM((3, 8, 64, 256), BF),
            pltpu.VMEM((4, 8, 16, 256), F32),
            pltpu.VMEM((4, 8, 16, 256), F32),
            pltpu.VMEM((3, 8, 16, 256), F32),
            pltpu.VMEM((3, 8, 16, 256), F32),
            pltpu.VMEM((2, 8, 2, 16, 256), BF),
            pltpu.VMEM((4, 2, 16, 16, 256), BF),
            pltpu.VMEM((2, 16, 4, 16, 256), BF),
            pltpu.VMEM((4, 2, 64, 1024), BF),
            pltpu.VMEM((4, 2, 64, 1024), BF),
            pltpu.VMEM((4, 64, 256), F32),
            pltpu.VMEM((4, 64, 256), F32),
            pltpu.VMEM((4, 2, 8, 128), F32),
            pltpu.VMEM((4, 2, 8, 128), F32),
            pltpu.VMEM((512, 128), F32),
            pltpu.VMEM((16, 32, 128), BF),
            pltpu.VMEM((16, 32, 128), BF),
            pltpu.VMEM((16, 32, 128), BF),
            pltpu.VMEM((64, 1024), F32),
            dma((6,)),
            dma((3, 4, 2)), dma((3, 4, 2)),
            dma((3, 4, 2)), dma((3, 4, 2)),
            dma((2, 8)), dma((8, 2)),
            dma((3,)), dma((3,)), dma((3,)), dma((3,)),
            dma((3,)), dma((3,)), dma((3,)), dma((3,)),
            dma((3,)), dma((3,)),
            dma((3,)), dma((3,)), dma((3,)), dma((3,)),
            dma((16,)), dma((16,)),
        ],
        compiler_params=pltpu.CompilerParams(
            collective_id=0, has_side_effects=True, vmem_limit_bytes=60 * 2**20
        ),
    )(grad_partial, owner_slots, jnp.swapaxes(left_roots, 1, 2), right_roots, momentum)
    return direction.reshape(16, 4, 1024), new_momentum


def solution(mesh):
    return jax.shard_map(
        body,
        mesh=mesh,
        in_specs=(
            P("dp", None, "shard", None),
            P(),
            P("shard", None, "dp"),
            P("shard", "dp", None),
            P("shard", "dp", None),
        ),
        out_specs=(P(None, ("dp", "shard"), None), P("shard", "dp", None)),
        check_vma=False,
    )
```

```python
import jax
import jax.numpy as jnp
from jax import lax
from jax.experimental import pallas as pl
from jax.experimental.pallas import tpu as pltpu
from jax.sharding import PartitionSpec as P

epsilon = 1e-06
decay_rate = 0.9

MESH = pl.DeviceIdType.MESH
BF = jnp.bfloat16
F32 = jnp.float32
CHUNKS = 4
OFFSETS = (4, 3, 5, 2, 6, 1, 7, 0)
PASS1 = (True, True, True, True, True, True, False, False)
PASS2 = (True, True, True, True, True, True, False, False)
PASSR = True
PASSL = True
NT = (((1,), (1,)), ((), ()))
NN = (((1,), (0,)), ((), ()))


def split(value):
    high = value.astype(BF)
    return high, (value - high.astype(F32)).astype(BF)


def dot(a, b, dims):
    return lax.dot_general(a, b, dims, preferred_element_type=F32)


def fold(value):
    rows = value.reshape(32, 8, 256).sum(axis=0)
    return rows[:, :128] + rows[:, 128:]


def kernel(
    gp, own, lr, rr, mo, dir_o, nm_o,
    gv, lv, rv, mv, stx, sty, r1x, r1y, s1x, s1y, r2x, r2y, zt, gbuf, hbuf, lg, rg,
    pt, pr, scx, scy, h32, hb, fin, ob, nm,
    loc, s1s, s1r, s2s, s2r, zs, zr, ls, lrc, rs, rrc, g1s, g1r, g2s, g2r, ts, tr,
    cxs, cxr, cys, cyr, fs, fr,
):
    dp = lax.axis_index("dp")
    shard = lax.axis_index("shard")
    x, y = lax.rem(dp, 4), lax.div(dp, 4)
    z, core = lax.div(shard, 2), lax.rem(shard, 2)
    u = (1 - core) * x + core * y
    v = (1 - core) * y + core * x

    def step(i, k):
        return lax.rem(i + k, 4)

    def to_x(k):
        return {"dp": y * 4 + step(x, k)}

    def to_y(k):
        return {"dp": step(y, k) * 4 + x}

    def to_u(k):
        return {"dp": (1 - core) * (y * 4 + step(x, k)) + core * (step(y, k) * 4 + x)}

    def to_v(k):
        return {"dp": core * (y * 4 + step(x, k)) + (1 - core) * (step(y, k) * 4 + x)}

    def remote(src, dst, ssem, rsem, device):
        return pltpu.make_async_remote_copy(
            src_ref=src, dst_ref=dst, send_sem=ssem, recv_sem=rsem, device_id=device, device_id_type=MESH
        )

    def start_all(copies):
        for copy in copies:
            copy.start()

    def recv_all(copies):
        for copy in copies:
            copy.wait_recv()

    def send_all(copies):
        for copy in copies:
            copy.wait_send()

    load_g = pltpu.make_async_copy(gp.at[0], gv, loc.at[0])
    load_l = pltpu.make_async_copy(lr.at[0], lv, loc.at[1])
    load_r = pltpu.make_async_copy(rr.at[0], rv, loc.at[2])
    load_m = pltpu.make_async_copy(mo.at[0], mv, loc.at[3])
    load_g.start()
    load_r.start()
    load_l.start()
    load_m.start()

    barrier = pltpu.get_barrier_semaphore()
    for k in range(1, 4):
        pl.semaphore_signal(barrier, inc=1, device_id=to_x(k), device_id_type=MESH)
        pl.semaphore_signal(barrier, inc=1, device_id=to_y(k), device_id_type=MESH)
    for k in range(1, 16):
        pl.semaphore_signal(
            barrier, inc=1, device_id={"shard": lax.rem(shard + k, 16)}, device_id_type=MESH
        )

    def block_of(slot):
        found = jnp.int32(0)
        for b in range(16):
            found = jnp.where(own[b] == slot, b, found)
        return found

    def stage(q):
        zq = lax.rem(z + OFFSETS[q], 8)
        for target, staged in enumerate((stx, sty)):
            block = gv[block_of(zq * 2 + target)]
            for i in range(4):
                staged[i, q] = block[16 * i : 16 * i + 16]

    def stage1(c):
        part = pl.ds(2 * c, 2)
        out = []
        for k in range(1, 4):
            out.append(remote(stx.at[step(x, k), part], r1x.at[k - 1, part], s1s.at[k - 1, c, 0], s1r.at[k - 1, c, 0], to_x(k)))
            out.append(remote(sty.at[step(y, k), part], r1y.at[k - 1, part], s1s.at[k - 1, c, 1], s1r.at[k - 1, c, 1], to_y(k)))
        return out

    def sum1(q):
        for staged, got, summed, me in ((stx, r1x, s1x, x), (sty, r1y, s1y, y)):
            total = staged[me, q].astype(F32)
            for k in range(3):
                total = total + got[k, q].astype(F32)
            for j in range(4):
                summed[j, q] = total[:, 256 * j : 256 * j + 256]

    def stage2(c):
        part = pl.ds(2 * c, 2)
        out = []
        for k in range(1, 4):
            out.append(remote(s1x.at[step(y, k), part], r2x.at[k - 1, part], s2s.at[k - 1, c, 0], s2r.at[k - 1, c, 0], to_y(k)))
            out.append(remote(s1y.at[step(x, k), part], r2y.at[k - 1, part], s2s.at[k - 1, c, 1], s2r.at[k - 1, c, 1], to_x(k)))
        return out

    def sum2(q):
        for target, (summed, got, me) in enumerate(((s1x, r2x, y), (s1y, r2y, x))):
            total = summed[me, q]
            for k in range(3):
                total = total + got[k, q]
            zt[target, q, 0], zt[target, q, 1] = split(total)

    def exchange(q, target):
        dst = gbuf.at[shard, y if target == 0 else x]
        device = {"shard": lax.rem(z + OFFSETS[q], 8) * 2 + target}
        return remote(zt.at[target, q], dst, zs.at[target, q], zr.at[q, core], device)

    def send_z(q):
        if OFFSETS[q]:
            exchange(q, 0).start()
            exchange(q, 1).start()
        else:
            @pl.when(core == 0)
            def _():
                exchange(q, 1).start()
                gbuf[shard, y] = zt[0, q]

            @pl.when(core == 1)
            def _():
                exchange(q, 0).start()
                gbuf[shard, x] = zt[1, q]

    def wait_z(q):
        for source in range(2):
            def wait():
                remote(zt.at[0, q], gbuf.at[shard, v], zs.at[0, q], zr.at[q, source], {"shard": shard}).wait_recv()

            if OFFSETS[q]:
                wait()
            else:
                pl.when(core != source)(wait)

    def sent_z(q):
        if OFFSETS[q]:
            exchange(q, 0).wait_send()
            exchange(q, 1).wait_send()
        else:
            pl.when(core == 0)(lambda: exchange(q, 1).wait_send())
            pl.when(core == 1)(lambda: exchange(q, 0).wait_send())

    def pair(q):
        return pl.ds(2 * lax.rem(z + 8 - OFFSETS[q], 8), 2)

    class Gather:
        def __init__(self, piece, half, me, to, ssem, rsem, passing):
            own_piece = piece(me)
            self.direct = [
                remote(own_piece, own_piece, ssem.at[0], rsem.at[0], to(1)),
                remote(own_piece, own_piece, ssem.at[1], rsem.at[1], to(3)),
            ]
            if passing:
                after, before = half(step(me, 3), 0), half(step(me, 1), 1)
                self.passed = [
                    remote(after, after, ssem.at[2], rsem.at[2], to(1)),
                    remote(before, before, ssem.at[3], rsem.at[3], to(3)),
                ]
            else:
                self.passed = [remote(own_piece, own_piece, ssem.at[2], rsem.at[2], to(2))]
            self.passing = passing

        def start(self):
            start_all(self.direct)
            if not self.passing:
                start_all(self.passed)

        def go_on(self):
            if self.passing:
                for received, onward in zip(self.direct, self.passed):
                    received.wait_recv()
                    onward.start()

        def wait(self):
            if not self.passing:
                recv_all(self.direct)
            recv_all(self.passed)

        def sent(self):
            send_all(self.direct)
            send_all(self.passed)

    def gather1(q):
        return Gather(
            lambda i: gbuf.at[pair(q), i], lambda i, h: gbuf.at[pair(q), i, h], v, to_v, g1s.at[q], g1r.at[q], PASS1[q]
        )

    def gather2(q):
        return Gather(
            lambda i: hbuf.at[:, pair(q), i], lambda i, h: hbuf.at[h, pair(q), i], u, to_u, g2s.at[q], g2r.at[q], PASS2[q]
        )

    def times_right(q):
        total = None
        for j in range(4):
            cols = slice(256 * j, 256 * j + 256)
            high, low = (
                jnp.concatenate([gbuf[pair(i), j, h].reshape(32, 256) for i in (q, q + 1)], axis=0) for h in range(2)
            )
            b_high = rg[:, 0, :, cols].reshape(256, 256)
            b_low = rg[:, 1, :, cols].reshape(256, 256)
            both = dot(jnp.concatenate([high, low], axis=0), b_high, NT)
            part = both[:64] + both[64:] + dot(high, b_low, NT)
            total = part if total is None else total + part
        high, low = split(total)
        for i in range(2):
            hbuf[0, pair(q + i), u] = high[32 * i : 32 * i + 32].reshape(2, 16, 256)
            hbuf[1, pair(q + i), u] = low[32 * i : 32 * i + 32].reshape(2, 16, 256)

    def left_times():
        a_high = lg[:, 0].reshape(256, 1024)
        a_low = lg[:, 1].reshape(256, 1024)
        b_high = hbuf[0].reshape(1024, 256)
        b_low = hbuf[1].reshape(1024, 256)
        return dot(a_high, b_high, NN) + dot(a_high, b_low, NN) + dot(a_low, b_high, NN)

    rights = Gather(lambda i: rg.at[i], lambda i, h: rg.at[i, h], u, to_u, rs, rrc, PASSR)
    lefts = Gather(lambda i: lg.at[i], lambda i, h: lg.at[i, h], v, to_v, ls, lrc, PASSL)

    load_g.wait()
    stage(0)
    stage(1)
    pl.semaphore_wait(barrier, 21)
    start_all(stage1(0))
    for c in range(1, CHUNKS):
        stage(2 * c)
        stage(2 * c + 1)
        start_all(stage1(c))

    load_r.wait()
    rg[u, 0], rg[u, 1] = split(rv[...])
    load_l.wait()
    lg[v, 0], lg[v, 1] = split(lv[...])

    def sum_first(c):
        recv_all(stage1(c))
        sum1(2 * c)
        sum1(2 * c + 1)
        start_all(stage2(c))

    def sum_second(c):
        recv_all(stage2(c))
        for q in (2 * c, 2 * c + 1):
            sum2(q)
            send_z(q)

    def spread_rows(c):
        for q in (2 * c, 2 * c + 1):
            wait_z(q)
            gather1(q).start()

    def pass_rows(c):
        for q in (2 * c, 2 * c + 1):
            gather1(q).go_on()

    def multiply_right(c):
        for q in (2 * c, 2 * c + 1):
            gather1(q).wait()
        times_right(2 * c)
        for q in (2 * c, 2 * c + 1):
            gather2(q).start()

    def pass_products(c):
        for q in (2 * c, 2 * c + 1):
            gather2(q).go_on()

    def wait_products(c):
        for q in (2 * c, 2 * c + 1):
            gather2(q).wait()

    def norm_of_gradient():
        tile = gbuf[:, v]
        tile = (tile[:, 0].astype(F32) + tile[:, 1].astype(F32)).reshape(256, 256)
        scx[x, 0] = fold(tile * tile)

    sum_first(0)
    sum_first(1)
    sum_first(2)
    sum_first(3)
    rights.start()
    sum_second(0)
    sum_second(1)
    sum_second(2)
    rights.go_on()
    sum_second(3)
    lefts.start()
    spread_rows(0)
    spread_rows(1)
    spread_rows(2)
    spread_rows(3)
    pass_rows(0)
    pass_rows(1)
    pass_rows(2)
    pass_rows(3)
    norm_of_gradient()
    lefts.go_on()
    rights.wait()
    multiply_right(0)
    multiply_right(1)
    multiply_right(2)
    multiply_right(3)
    pass_products(0)
    pass_products(1)
    pass_products(2)
    pass_products(3)
    lefts.wait()
    wait_products(0)
    wait_products(1)
    wait_products(2)
    wait_products(3)

    tile = left_times()
    scx[x, 1] = fold(tile * tile)
    for j in range(4):
        pt[j] = tile[64 * j : 64 * j + 64]

    norms_x = [remote(scx.at[x], scx.at[x], cxs.at[k - 1], cxr.at[k - 1], to_x(k)) for k in range(1, 4)]
    norms_y = [remote(scy.at[y], scy.at[y], cys.at[k - 1], cyr.at[k - 1], to_y(k)) for k in range(1, 4)]
    turn = [remote(pt.at[step(v, k)], pr.at[v], ts.at[k - 1], tr.at[k - 1], to_v(k)) for k in range(1, 4)]
    start_all(norms_x)
    start_all(turn)
    pr[v] = pt[v]
    load_m.wait()
    for c in range(CHUNKS):
        send_all(stage1(c))
    recv_all(norms_x)
    scy[y] = scx[0] + scx[1] + scx[2] + scx[3]
    start_all(norms_y)
    for c in range(CHUNKS):
        send_all(stage2(c))
    for q in range(8):
        sent_z(q)
    recv_all(turn)
    recv_all(norms_y)
    sums = scy[0] + scy[1] + scy[2] + scy[3]
    entries = 1024 * 1024
    grad_total = jnp.sum(sums[0], keepdims=True)
    prec_total = jnp.sum(sums[1], keepdims=True)
    scale = jnp.sqrt(grad_total / entries + epsilon) / jnp.sqrt(prec_total / entries + epsilon)

    def update(columns):
        for j in range(8):
            cols = slice(128 * j, 128 * j + 128)
            graft = columns(j) * scale
            moved = decay_rate * mv[:, cols] + graft
            nm[:, cols] = moved
            h32[:, cols] = decay_rate * moved + graft

    @pl.when(core == 0)
    def _():
        update(lambda j: pr[j // 2, :, 128 * (j % 2) : 128 * (j % 2) + 128])

    @pl.when(core == 1)
    def _():
        def columns(j):
            strip = slice(64 * (j // 2), 64 * (j // 2) + 64)
            first = 2 * (j % 2)
            return jnp.concatenate([pr[first, :, strip], pr[first + 1, :, strip]], axis=1)

        update(columns)

    hb[...] = h32[...].reshape(16, 4, 1024).astype(BF)

    def back(k):
        to = lax.rem(shard + k, 16)
        return remote(hb.at[to], fin.at[shard], fs.at[k], fr.at[k], {"shard": to})

    order = (8, 9, 7, 10, 6, 11, 5, 12, 4, 13, 3, 14, 2, 15, 1)
    for k in order:
        back(k).start()
    store_m = pltpu.make_async_copy(nm, nm_o.at[0], loc.at[4])
    store_m.start()
    fin[shard] = hb[shard]
    send_all(norms_x)
    send_all(norms_y)
    send_all(turn)
    rights.sent()
    lefts.sent()
    for q in range(8):
        gather1(q).sent()
        gather2(q).sent()
    for k in order:
        back(k).wait_recv()
    for b in range(16):
        ob[b] = fin[own[b]]
    store_d = pltpu.make_async_copy(ob, dir_o, loc.at[5])
    store_d.start()
    for k in order:
        back(k).wait_send()
    store_m.wait()
    store_d.wait()


def last(d_in, m_in, d_out, m_out, sem, d, m):
    loads = [pltpu.make_async_copy(m_in, m, sem.at[0]), pltpu.make_async_copy(d_in, d, sem.at[1])]
    stores = [pltpu.make_async_copy(m, m_out, sem.at[2]), pltpu.make_async_copy(d, d_out, sem.at[3])]
    for copy in loads:
        copy.start()
    for load, store in zip(loads, stores):
        load.wait()
        store.start()
    for copy in stores:
        copy.wait()


def body(grad_partial, owner_slots, left_roots, right_roots, momentum):
    dma = pltpu.SemaphoreType.DMA
    any_space = pl.BlockSpec(memory_space=pl.ANY)
    direction, new_momentum = pl.pallas_call(
        kernel,
        out_shape=(
            jax.ShapeDtypeStruct((16, 4, 1024), BF),
            jax.ShapeDtypeStruct((1, 64, 1024), F32),
        ),
        in_specs=[any_space, pl.BlockSpec(memory_space=pltpu.SMEM), any_space, any_space, any_space],
        out_specs=(any_space, any_space),
        scratch_shapes=[
            pltpu.VMEM((16, 64, 1024), BF),
            pltpu.VMEM((64, 1024), F32),
            pltpu.VMEM((64, 1024), F32),
            pltpu.VMEM((64, 1024), F32),
            pltpu.VMEM((4, 8, 16, 1024), BF),
            pltpu.VMEM((4, 8, 16, 1024), BF),
            pltpu.VMEM((3, 8, 16, 1024), BF),
            pltpu.VMEM((3, 8, 16, 1024), BF),
            pltpu.VMEM((4, 8, 16, 256), F32),
            pltpu.VMEM((4, 8, 16, 256), F32),
            pltpu.VMEM((3, 8, 16, 256), F32),
            pltpu.VMEM((3, 8, 16, 256), F32),
            pltpu.VMEM((2, 8, 2, 16, 256), BF),
            pltpu.VMEM((16, 4, 2, 16, 256), BF),
            pltpu.VMEM((2, 16, 4, 16, 256), BF),
            pltpu.VMEM((4, 2, 64, 1024), BF),
            pltpu.VMEM((4, 2, 64, 1024), BF),
            pltpu.VMEM((4, 64, 256), F32),
            pltpu.VMEM((4, 64, 256), F32),
            pltpu.VMEM((4, 2, 8, 128), F32),
            pltpu.VMEM((4, 2, 8, 128), F32),
            pltpu.VMEM((64, 1024), F32),
            pltpu.VMEM((16, 4, 1024), BF),
            pltpu.VMEM((16, 4, 1024), BF),
            pltpu.VMEM((16, 4, 1024), BF),
            pltpu.VMEM((64, 1024), F32),
            dma((6,)),
            dma((3, 4, 2)), dma((3, 4, 2)),
            dma((3, 4, 2)), dma((3, 4, 2)),
            dma((2, 8)), dma((8, 2)),
            dma((4,)), dma((4,)), dma((4,)), dma((4,)),
            dma((8, 4)), dma((8, 4)), dma((8, 4)), dma((8, 4)),
            dma((3,)), dma((3,)),
            dma((3,)), dma((3,)), dma((3,)), dma((3,)),
            dma((16,)), dma((16,)),
        ],
        compiler_params=pltpu.CompilerParams(
            collective_id=0, has_side_effects=True, vmem_limit_bytes=60 * 2**20
        ),
    )(grad_partial, owner_slots, jnp.swapaxes(left_roots, 1, 2), right_roots, momentum)
    vmem = pl.BlockSpec(memory_space=pltpu.VMEM)
    return pl.pallas_call(
        last,
        out_shape=(
            jax.ShapeDtypeStruct((16, 4, 1024), BF),
            jax.ShapeDtypeStruct((1, 64, 1024), F32),
        ),
        in_specs=[any_space, any_space],
        out_specs=(any_space, any_space),
        scratch_shapes=[dma((4,)), pltpu.VMEM((16, 4, 1024), BF), pltpu.VMEM((1, 64, 1024), F32)],
        compiler_params=pltpu.CompilerParams(vmem_limit_bytes=60 * 2**20),
    )(direction, new_momentum)


def solution(mesh):
    return jax.shard_map(
        body,
        mesh=mesh,
        in_specs=(
            P("dp", None, "shard", None),
            P(),
            P("shard", None, "dp"),
            P("shard", "dp", None),
            P("shard", "dp", None),
        ),
        out_specs=(P(None, ("dp", "shard"), None), P("shard", "dp", None)),
        check_vma=False,
    )
```

```python
import jax
import jax.numpy as jnp
from jax import lax
from jax.experimental import pallas as pl
from jax.experimental.pallas import tpu as pltpu
from jax.sharding import PartitionSpec as P

epsilon = 1e-06
decay_rate = 0.9

MESH = pl.DeviceIdType.MESH
BF = jnp.bfloat16
F32 = jnp.float32
PARTS = ((0, 2), (2, 2), (4, 2), (6, 2))
CHUNKS = len(PARTS)
OFFSETS = (4, 3, 5, 2, 6, 1, 7, 0)
PASS1 = (True, True, True, True, True, True, False, False)
PASS2 = (True, True, True, True, True, True, False, False)
PASSR = True
PASSL = True
NT = (((1,), (1,)), ((), ()))
NN = (((1,), (0,)), ((), ()))


def split(value):
    high = value.astype(BF)
    return high, (value - high.astype(F32)).astype(BF)


def dot(a, b, dims):
    return lax.dot_general(a, b, dims, preferred_element_type=F32)


def fold(value):
    rows = value.reshape(32, 8, 256).sum(axis=0)
    return rows[:, :128] + rows[:, 128:]


def kernel(
    gp, own, lr, rr, mo, dir_o, nm_o,
    gv, lv, rv, mv, stx, sty, r1x, r1y, s1x, s1y, r2x, r2y, zt, gbuf, hbuf, lg, rg,
    pt, pr, scx, scy, h32, hb, fin, ob, nm,
    loc, s1s, s1r, s2s, s2r, zs, zr, ls, lrc, rs, rrc, g1s, g1r, g2s, g2r, ts, tr,
    cxs, cxr, cys, cyr, fs, fr,
):
    dp = lax.axis_index("dp")
    shard = lax.axis_index("shard")
    x, y = lax.rem(dp, 4), lax.div(dp, 4)
    z, core = lax.div(shard, 2), lax.rem(shard, 2)
    u = (1 - core) * x + core * y
    v = (1 - core) * y + core * x

    def step(i, k):
        return lax.rem(i + k, 4)

    def to_x(k):
        return {"dp": y * 4 + step(x, k)}

    def to_y(k):
        return {"dp": step(y, k) * 4 + x}

    def to_u(k):
        return {"dp": (1 - core) * (y * 4 + step(x, k)) + core * (step(y, k) * 4 + x)}

    def to_v(k):
        return {"dp": core * (y * 4 + step(x, k)) + (1 - core) * (step(y, k) * 4 + x)}

    def remote(src, dst, ssem, rsem, device):
        return pltpu.make_async_remote_copy(
            src_ref=src, dst_ref=dst, send_sem=ssem, recv_sem=rsem, device_id=device, device_id_type=MESH
        )

    def start_all(copies):
        for copy in copies:
            copy.start()

    def recv_all(copies):
        for copy in copies:
            copy.wait_recv()

    def send_all(copies):
        for copy in copies:
            copy.wait_send()

    load_g = pltpu.make_async_copy(gp.at[0], gv, loc.at[0])
    load_l = pltpu.make_async_copy(lr.at[0], lv, loc.at[1])
    load_r = pltpu.make_async_copy(rr.at[0], rv, loc.at[2])
    load_m = pltpu.make_async_copy(mo.at[0], mv, loc.at[3])
    load_g.start()
    load_r.start()
    load_l.start()
    load_m.start()

    barrier = pltpu.get_barrier_semaphore()
    for k in range(1, 4):
        pl.semaphore_signal(barrier, inc=1, device_id=to_x(k), device_id_type=MESH)
        pl.semaphore_signal(barrier, inc=1, device_id=to_y(k), device_id_type=MESH)
    for k in range(1, 16):
        pl.semaphore_signal(
            barrier, inc=1, device_id={"shard": lax.rem(shard + k, 16)}, device_id_type=MESH
        )

    def block_of(slot):
        found = jnp.int32(0)
        for b in range(16):
            found = jnp.where(own[b] == slot, b, found)
        return found

    def stage(q):
        zq = lax.rem(z + OFFSETS[q], 8)
        for target, staged in enumerate((stx, sty)):
            block = gv[block_of(zq * 2 + target)]
            for i in range(4):
                staged[i, q] = block[16 * i : 16 * i + 16]

    def stage1(c):
        part = pl.ds(*PARTS[c])
        out = []
        for k in range(1, 4):
            out.append(remote(stx.at[step(x, k), part], r1x.at[k - 1, part], s1s.at[k - 1, c, 0], s1r.at[k - 1, c, 0], to_x(k)))
            out.append(remote(sty.at[step(y, k), part], r1y.at[k - 1, part], s1s.at[k - 1, c, 1], s1r.at[k - 1, c, 1], to_y(k)))
        return out

    def sum1(q):
        for staged, got, summed, me in ((stx, r1x, s1x, x), (sty, r1y, s1y, y)):
            total = staged[me, q].astype(F32)
            for k in range(3):
                total = total + got[k, q].astype(F32)
            for j in range(4):
                summed[j, q] = total[:, 256 * j : 256 * j + 256]

    def stage2(c):
        part = pl.ds(*PARTS[c])
        out = []
        for k in range(1, 4):
            out.append(remote(s1x.at[step(y, k), part], r2x.at[k - 1, part], s2s.at[k - 1, c, 0], s2r.at[k - 1, c, 0], to_y(k)))
            out.append(remote(s1y.at[step(x, k), part], r2y.at[k - 1, part], s2s.at[k - 1, c, 1], s2r.at[k - 1, c, 1], to_x(k)))
        return out

    def sum2(q):
        for target, (summed, got, me) in enumerate(((s1x, r2x, y), (s1y, r2y, x))):
            total = summed[me, q]
            for k in range(3):
                total = total + got[k, q]
            zt[target, q, 0], zt[target, q, 1] = split(total)

    def exchange(q, target):
        dst = gbuf.at[shard, y if target == 0 else x]
        device = {"shard": lax.rem(z + OFFSETS[q], 8) * 2 + target}
        return remote(zt.at[target, q], dst, zs.at[target, q], zr.at[q, core], device)

    def send_z(q):
        if OFFSETS[q]:
            exchange(q, 0).start()
            exchange(q, 1).start()
        else:
            @pl.when(core == 0)
            def _():
                exchange(q, 1).start()
                gbuf[shard, y] = zt[0, q]

            @pl.when(core == 1)
            def _():
                exchange(q, 0).start()
                gbuf[shard, x] = zt[1, q]

    def wait_z(q):
        for source in range(2):
            def wait():
                remote(zt.at[0, q], gbuf.at[shard, v], zs.at[0, q], zr.at[q, source], {"shard": shard}).wait_recv()

            if OFFSETS[q]:
                wait()
            else:
                pl.when(core != source)(wait)

    def sent_z(q):
        if OFFSETS[q]:
            exchange(q, 0).wait_send()
            exchange(q, 1).wait_send()
        else:
            pl.when(core == 0)(lambda: exchange(q, 1).wait_send())
            pl.when(core == 1)(lambda: exchange(q, 0).wait_send())

    def pair(q):
        return pl.ds(2 * lax.rem(z + 8 - OFFSETS[q], 8), 2)

    class Gather:
        def __init__(self, piece, half, me, to, ssem, rsem, passing):
            own_piece = piece(me)
            self.direct = [
                remote(own_piece, own_piece, ssem.at[0], rsem.at[0], to(1)),
                remote(own_piece, own_piece, ssem.at[1], rsem.at[1], to(3)),
            ]
            if passing:
                after, before = half(step(me, 3), 0), half(step(me, 1), 1)
                self.passed = [
                    remote(after, after, ssem.at[2], rsem.at[2], to(1)),
                    remote(before, before, ssem.at[3], rsem.at[3], to(3)),
                ]
            else:
                self.passed = [remote(own_piece, own_piece, ssem.at[2], rsem.at[2], to(2))]
            self.passing = passing

        def start(self):
            start_all(self.direct)
            if not self.passing:
                start_all(self.passed)

        def go_on(self):
            if self.passing:
                for received, onward in zip(self.direct, self.passed):
                    received.wait_recv()
                    start_all([onward])

        def wait(self):
            if not self.passing:
                recv_all(self.direct)
            recv_all(self.passed)

        def sent(self):
            send_all(self.direct)
            send_all(self.passed)

    def gather1(q):
        return Gather(
            lambda i: gbuf.at[pair(q), i], lambda i, h: gbuf.at[pair(q), i, h], v, to_v, g1s.at[q], g1r.at[q], PASS1[q]
        )

    def gather2(q):
        return Gather(
            lambda i: hbuf.at[:, pair(q), i], lambda i, h: hbuf.at[h, pair(q), i], u, to_u, g2s.at[q], g2r.at[q], PASS2[q]
        )

    def times_right(qs):
        rows = 32 * len(qs)
        total = None
        for j in range(4):
            cols = slice(256 * j, 256 * j + 256)
            high, low = (
                jnp.concatenate([gbuf[pair(i), j, h].reshape(32, 256) for i in qs], axis=0) for h in range(2)
            )
            b_high = rg[:, 0, :, cols].reshape(256, 256)
            b_low = rg[:, 1, :, cols].reshape(256, 256)
            both = dot(jnp.concatenate([high, low], axis=0), b_high, NT)
            part = both[:rows] + both[rows:] + dot(high, b_low, NT)
            total = part if total is None else total + part
        high, low = split(total)
        for i, q in enumerate(qs):
            hbuf[0, pair(q), u] = high[32 * i : 32 * i + 32].reshape(2, 16, 256)
            hbuf[1, pair(q), u] = low[32 * i : 32 * i + 32].reshape(2, 16, 256)

    def left_times(part):
        high, low = [], []
        for q in part:
            cols = pl.ds(pl.multiple_of(128 * lax.rem(z + 8 - OFFSETS[q], 8), 128), 128)
            high.append(lg[:, 0, :, cols].reshape(256, 128))
            low.append(lg[:, 1, :, cols].reshape(256, 128))
        a_high, a_low = (jnp.concatenate(cols, axis=1) for cols in (high, low))
        b_high, b_low = (
            jnp.concatenate([hbuf[h, pair(q)].reshape(128, 256) for q in part], axis=0) for h in range(2)
        )
        return dot(a_high, b_high, NN) + dot(a_high, b_low, NN) + dot(a_low, b_high, NN)

    rights = Gather(lambda i: rg.at[i], lambda i, h: rg.at[i, h], u, to_u, rs, rrc, PASSR)
    lefts = Gather(lambda i: lg.at[i], lambda i, h: lg.at[i, h], v, to_v, ls, lrc, PASSL)

    def slots(c):
        return range(PARTS[c][0], PARTS[c][0] + PARTS[c][1])

    load_g.wait()
    for c in range(CHUNKS):
        for q in slots(c):
            stage(q)
        if c == 0:
            pl.semaphore_wait(barrier, 21)
        start_all(stage1(c))

    load_r.wait()
    rg[u, 0], rg[u, 1] = split(rv[...])
    load_l.wait()
    lg[v, 0], lg[v, 1] = split(lv[...])

    def sum_first(c):
        recv_all(stage1(c))
        for q in slots(c):
            sum1(q)
        start_all(stage2(c))

    def sum_second(c):
        recv_all(stage2(c))
        for q in slots(c):
            sum2(q)
            send_z(q)

    def spread_rows(c):
        for q in slots(c):
            wait_z(q)
            gather1(q).start()

    def pass_rows(c):
        for q in slots(c):
            gather1(q).go_on()

    def multiply_right(c):
        for q in slots(c):
            gather1(q).wait()
        times_right(slots(c))
        for q in slots(c):
            gather2(q).start()

    def pass_products(c):
        for q in slots(c):
            gather2(q).go_on()

    def multiply_left(c):
        for q in slots(c):
            gather2(q).wait()
        product = left_times(slots(c)).reshape(4, 64, 256)
        pt[...] = product if c == 0 else pt[...] + product

    def norm_of_gradient():
        tile = gbuf[:, v]
        tile = (tile[:, 0].astype(F32) + tile[:, 1].astype(F32)).reshape(256, 256)
        scx[x, 0] = fold(tile * tile)

    sum_first(0)
    sum_first(1)
    sum_first(2)
    sum_first(3)
    rights.start()
    sum_second(0)
    sum_second(1)
    sum_second(2)
    rights.go_on()
    sum_second(3)
    lefts.start()
    spread_rows(0)
    spread_rows(1)
    spread_rows(2)
    spread_rows(3)
    pass_rows(0)
    pass_rows(1)
    pass_rows(2)
    pass_rows(3)
    norm_of_gradient()
    lefts.go_on()
    rights.wait()
    multiply_right(0)
    multiply_right(1)
    multiply_right(2)
    multiply_right(3)
    pass_products(0)
    pass_products(1)
    pass_products(2)
    pass_products(3)
    lefts.wait()
    multiply_left(0)
    multiply_left(1)
    multiply_left(2)
    multiply_left(3)

    tile = pt[...].reshape(256, 256)
    scx[x, 1] = fold(tile * tile)

    norms_x = [remote(scx.at[x], scx.at[x], cxs.at[k - 1], cxr.at[k - 1], to_x(k)) for k in range(1, 4)]
    norms_y = [remote(scy.at[y], scy.at[y], cys.at[k - 1], cyr.at[k - 1], to_y(k)) for k in range(1, 4)]
    turn = [remote(pt.at[step(v, k)], pr.at[v], ts.at[k - 1], tr.at[k - 1], to_v(k)) for k in range(1, 4)]
    start_all(norms_x)
    start_all(turn)
    pr[v] = pt[v]
    load_m.wait()
    for c in range(CHUNKS):
        send_all(stage1(c))
    recv_all(norms_x)
    scy[y] = scx[0] + scx[1] + scx[2] + scx[3]
    start_all(norms_y)
    for c in range(CHUNKS):
        send_all(stage2(c))
    for q in range(8):
        sent_z(q)
    recv_all(turn)
    recv_all(norms_y)
    sums = scy[0] + scy[1] + scy[2] + scy[3]
    entries = 1024 * 1024
    grad_total = jnp.sum(sums[0], keepdims=True)
    prec_total = jnp.sum(sums[1], keepdims=True)
    scale = jnp.sqrt(grad_total / entries + epsilon) / jnp.sqrt(prec_total / entries + epsilon)

    def update(columns):
        for j in range(8):
            cols = slice(128 * j, 128 * j + 128)
            graft = columns(j) * scale
            moved = decay_rate * mv[:, cols] + graft
            nm_o[0, :, cols] = moved
            h32[:, cols] = decay_rate * moved + graft

    @pl.when(core == 0)
    def _():
        update(lambda j: pr[j // 2, :, 128 * (j % 2) : 128 * (j % 2) + 128])

    @pl.when(core == 1)
    def _():
        def columns(j):
            strip = slice(64 * (j // 2), 64 * (j // 2) + 64)
            first = 2 * (j % 2)
            return jnp.concatenate([pr[first, :, strip], pr[first + 1, :, strip]], axis=1)

        update(columns)

    hb[...] = h32[...].reshape(16, 4, 1024).astype(BF)

    def back(k):
        to = lax.rem(shard + k, 16)
        return remote(hb.at[to], fin.at[shard], fs.at[k], fr.at[k], {"shard": to})

    order = (8, 9, 7, 10, 6, 11, 5, 12, 4, 13, 3, 14, 2, 15, 1)
    for k in order:
        back(k).start()
    fin[shard] = hb[shard]
    send_all(norms_x)
    send_all(norms_y)
    send_all(turn)
    rights.sent()
    lefts.sent()
    for q in range(8):
        gather1(q).sent()
        gather2(q).sent()
    for k in order:
        back(k).wait_recv()
    for b in range(16):
        dir_o[b] = fin[own[b]]
    for k in order:
        back(k).wait_send()


def last(d_in, m_in, d_out, m_out, sem):
    copies = [pltpu.make_async_copy(m_in, m_out, sem.at[0]), pltpu.make_async_copy(d_in, d_out, sem.at[1])]
    for copy in copies:
        copy.start()
    for copy in copies:
        copy.wait()


def body(grad_partial, owner_slots, left_roots, right_roots, momentum):
    dma = pltpu.SemaphoreType.DMA
    any_space = pl.BlockSpec(memory_space=pl.ANY)
    direction, new_momentum = pl.pallas_call(
        kernel,
        out_shape=(
            jax.ShapeDtypeStruct((16, 4, 1024), BF),
            jax.ShapeDtypeStruct((1, 64, 1024), F32),
        ),
        in_specs=[any_space, pl.BlockSpec(memory_space=pltpu.SMEM), any_space, any_space, any_space],
        out_specs=(pl.BlockSpec(memory_space=pltpu.VMEM),) * 2,
        scratch_shapes=[
            pltpu.VMEM((16, 64, 1024), BF),
            pltpu.VMEM((64, 1024), F32),
            pltpu.VMEM((64, 1024), F32),
            pltpu.VMEM((64, 1024), F32),
            pltpu.VMEM((4, 8, 16, 1024), BF),
            pltpu.VMEM((4, 8, 16, 1024), BF),
            pltpu.VMEM((3, 8, 16, 1024), BF),
            pltpu.VMEM((3, 8, 16, 1024), BF),
            pltpu.VMEM((4, 8, 16, 256), F32),
            pltpu.VMEM((4, 8, 16, 256), F32),
            pltpu.VMEM((3, 8, 16, 256), F32),
            pltpu.VMEM((3, 8, 16, 256), F32),
            pltpu.VMEM((2, 8, 2, 16, 256), BF),
            pltpu.VMEM((16, 4, 2, 16, 256), BF),
            pltpu.VMEM((2, 16, 4, 16, 256), BF),
            pltpu.VMEM((4, 2, 64, 1024), BF),
            pltpu.VMEM((4, 2, 64, 1024), BF),
            pltpu.VMEM((4, 64, 256), F32),
            pltpu.VMEM((4, 64, 256), F32),
            pltpu.VMEM((4, 2, 8, 128), F32),
            pltpu.VMEM((4, 2, 8, 128), F32),
            pltpu.VMEM((64, 1024), F32),
            pltpu.VMEM((16, 4, 1024), BF),
            pltpu.VMEM((16, 4, 1024), BF),
            pltpu.VMEM((16, 4, 1024), BF),
            pltpu.VMEM((64, 1024), F32),
            dma((6,)),
            dma((3, CHUNKS, 2)), dma((3, CHUNKS, 2)),
            dma((3, CHUNKS, 2)), dma((3, CHUNKS, 2)),
            dma((2, 8)), dma((8, 2)),
            dma((4,)), dma((4,)), dma((4,)), dma((4,)),
            dma((8, 4)), dma((8, 4)), dma((8, 4)), dma((8, 4)),
            dma((3,)), dma((3,)),
            dma((3,)), dma((3,)), dma((3,)), dma((3,)),
            dma((16,)), dma((16,)),
        ],
        compiler_params=pltpu.CompilerParams(
            collective_id=0, has_side_effects=True, vmem_limit_bytes=54800 * 1024
        ),
    )(grad_partial, owner_slots, jnp.swapaxes(left_roots, 1, 2), right_roots, momentum)
    vmem = pl.BlockSpec(memory_space=pltpu.VMEM)
    return pl.pallas_call(
        last,
        out_shape=(
            jax.ShapeDtypeStruct((16, 4, 1024), BF),
            jax.ShapeDtypeStruct((1, 64, 1024), F32),
        ),
        in_specs=[vmem, vmem],
        out_specs=(any_space, any_space),
        scratch_shapes=[dma((2,))],
        compiler_params=pltpu.CompilerParams(vmem_limit_bytes=2 * 2**20),
    )(direction, new_momentum)


def solution(mesh):
    return jax.shard_map(
        body,
        mesh=mesh,
        in_specs=(
            P("dp", None, "shard", None),
            P(),
            P("shard", None, "dp"),
            P("shard", "dp", None),
            P("shard", "dp", None),
        ),
        out_specs=(P(None, ("dp", "shard"), None), P("shard", "dp", None)),
        check_vma=False,
    )
```

```python
import jax
import jax.numpy as jnp
from jax import lax
from jax.experimental import pallas as pl
from jax.experimental.pallas import tpu as pltpu
from jax.sharding import PartitionSpec as P

epsilon = 1e-06
decay_rate = 0.9

MESH = pl.DeviceIdType.MESH
BF = jnp.bfloat16
F32 = jnp.float32
PARTS = ((0, 2), (2, 2), (4, 1), (5, 3))
EARLY = 5
CHUNKS = len(PARTS) - 1
OFFSETS = (4, 3, 5, 2, 6, 1, 7, 0)
PASS1 = (True,) * 5 + (False,) * 3
PASS2 = (True,) * 5 + (False,) * 3
PASSR = True
PASSL = True
NT = (((1,), (1,)), ((), ()))
NN = (((1,), (0,)), ((), ()))


def split(value):
    high = value.astype(BF)
    return high, (value - high.astype(F32)).astype(BF)


def dot(a, b, dims):
    return lax.dot_general(a, b, dims, preferred_element_type=F32)


def fold(value):
    rows = value.reshape(32, 8, 256).sum(axis=0)
    return rows[:, :128] + rows[:, 128:]


def kernel(
    gp, own, lr, rr, mo, dir_o, nm_o,
    gv, lv, rv, mv, stx, sty, r1x, r1y, s1x, s1y, r2x, r2y, ez, r1e, s1e, r2e, zt, gbuf, hbuf, lg, rg,
    pt, pr, scx, scy, h32, hb, fin, ob, nm,
    loc, es, er, e1s, e1r, e2s, e2r, s1s, s1r, s2s, s2r, zs, zr, ls, lrc, rs, rrc, g1s, g1r, g2s, g2r, ts, tr,
    cxs, cxr, cys, cyr, fs, fr,
):
    dp = lax.axis_index("dp")
    shard = lax.axis_index("shard")
    x, y = lax.rem(dp, 4), lax.div(dp, 4)
    z, core = lax.div(shard, 2), lax.rem(shard, 2)
    u = (1 - core) * x + core * y
    v = (1 - core) * y + core * x

    def step(i, k):
        return lax.rem(i + k, 4)

    def to_x(k):
        return {"dp": y * 4 + step(x, k)}

    def to_y(k):
        return {"dp": step(y, k) * 4 + x}

    def to_u(k):
        return {"dp": (1 - core) * (y * 4 + step(x, k)) + core * (step(y, k) * 4 + x)}

    def to_v(k):
        return {"dp": core * (y * 4 + step(x, k)) + (1 - core) * (step(y, k) * 4 + x)}

    def remote(src, dst, ssem, rsem, device):
        return pltpu.make_async_remote_copy(
            src_ref=src, dst_ref=dst, send_sem=ssem, recv_sem=rsem, device_id=device, device_id_type=MESH
        )

    def start_all(copies):
        for copy in copies:
            copy.start()

    def recv_all(copies):
        for copy in copies:
            copy.wait_recv()

    def send_all(copies):
        for copy in copies:
            copy.wait_send()

    load_g = pltpu.make_async_copy(gp.at[0], gv, loc.at[0])
    load_l = pltpu.make_async_copy(lr.at[0], lv, loc.at[1])
    load_r = pltpu.make_async_copy(rr.at[0], rv, loc.at[2])
    load_m = pltpu.make_async_copy(mo.at[0], mv, loc.at[3])
    load_g.start()
    load_r.start()
    load_l.start()
    load_m.start()

    barrier = pltpu.get_barrier_semaphore()
    for k in range(1, 4):
        pl.semaphore_signal(barrier, inc=1, device_id=to_x(k), device_id_type=MESH)
        pl.semaphore_signal(barrier, inc=1, device_id=to_y(k), device_id_type=MESH)
    for k in range(1, 16):
        pl.semaphore_signal(
            barrier, inc=1, device_id={"shard": lax.rem(shard + k, 16)}, device_id_type=MESH
        )

    def block_of(slot):
        found = jnp.int32(0)
        for b in range(16):
            found = jnp.where(own[b] == slot, b, found)
        return found

    def stage(q):
        zq = lax.rem(z + OFFSETS[q], 8)
        for target, staged in enumerate((stx, sty)):
            block = gv[block_of(zq * 2 + target)]
            for i in range(4):
                staged[i, q] = block[16 * i : 16 * i + 16]

    def stage1(c):
        part = pl.ds(*PARTS[c])
        out = []
        for k in range(1, 4):
            out.append(remote(stx.at[step(x, k), part], r1x.at[k - 1, part], s1s.at[k - 1, c, 0], s1r.at[k - 1, c, 0], to_x(k)))
            out.append(remote(sty.at[step(y, k), part], r1y.at[k - 1, part], s1s.at[k - 1, c, 1], s1r.at[k - 1, c, 1], to_y(k)))
        return out

    def sum1(q):
        for staged, got, summed, me in ((stx, r1x, s1x, x), (sty, r1y, s1y, y)):
            total = staged[me, q].astype(F32)
            for k in range(3):
                total = total + got[k, q].astype(F32)
            for j in range(4):
                summed[j, q] = total[:, 256 * j : 256 * j + 256]

    def stage2(c):
        part = pl.ds(*PARTS[c])
        out = []
        for k in range(1, 4):
            out.append(remote(s1x.at[step(y, k), part], r2x.at[k - 1, part], s2s.at[k - 1, c, 0], s2r.at[k - 1, c, 0], to_y(k)))
            out.append(remote(s1y.at[step(x, k), part], r2y.at[k - 1, part], s2s.at[k - 1, c, 1], s2r.at[k - 1, c, 1], to_x(k)))
        return out

    def sum2(q):
        for target, (summed, got, me) in enumerate(((s1x, r2x, y), (s1y, r2y, x))):
            total = summed[me, q]
            for k in range(3):
                total = total + got[k, q]
            zt[target, q, 0], zt[target, q, 1] = split(total)

    def exchange(q, target):
        dst = gbuf.at[shard, y if target == 0 else x]
        device = {"shard": lax.rem(z + OFFSETS[q], 8) * 2 + target}
        return remote(zt.at[target, q], dst, zs.at[target, q], zr.at[q, core], device)

    def send_z(q):
        if OFFSETS[q]:
            exchange(q, 0).start()
            exchange(q, 1).start()
        else:
            @pl.when(core == 0)
            def _():
                exchange(q, 1).start()
                gbuf[shard, y] = zt[0, q]

            @pl.when(core == 1)
            def _():
                exchange(q, 0).start()
                gbuf[shard, x] = zt[1, q]

    def wait_z(q):
        for source in range(2):
            def wait():
                remote(zt.at[0, q], gbuf.at[shard, v], zs.at[0, q], zr.at[q, source], {"shard": shard}).wait_recv()

            if OFFSETS[q]:
                wait()
            else:
                pl.when(core != source)(wait)

    def sent_z(q):
        if OFFSETS[q]:
            exchange(q, 0).wait_send()
            exchange(q, 1).wait_send()
        else:
            pl.when(core == 0)(lambda: exchange(q, 1).wait_send())
            pl.when(core == 1)(lambda: exchange(q, 0).wait_send())

    def early(q, target):
        staged = (stx, sty)[target]
        e = q - EARLY
        device = {"shard": lax.rem(z + OFFSETS[q], 8) * 2 + target}
        return remote(staged.at[:, q], ez.at[:, 2 * e + core], es.at[target, e], er.at[e, core], device)

    def send_early(q):
        if OFFSETS[q]:
            early(q, 0).start()
            early(q, 1).start()
        else:
            @pl.when(core == 0)
            def _():
                early(q, 1).start()
                ez[:, 2 * (q - EARLY)] = stx[:, q]

            @pl.when(core == 1)
            def _():
                early(q, 0).start()
                ez[:, 2 * (q - EARLY) + 1] = sty[:, q]

    def wait_early(q):
        e = q - EARLY
        for source in range(2):
            def wait():
                remote(stx.at[:, q], ez.at[:, 2 * e + source], es.at[0, e], er.at[e, source], {"shard": shard}).wait_recv()

            if OFFSETS[q]:
                wait()
            else:
                pl.when(core != source)(wait)

    def sent_early(q):
        if OFFSETS[q]:
            early(q, 0).wait_send()
            early(q, 1).wait_send()
        else:
            pl.when(core == 0)(lambda: early(q, 1).wait_send())
            pl.when(core == 1)(lambda: early(q, 0).wait_send())

    def early1(q):
        e = q - EARLY
        part = pl.ds(2 * e, 2)
        return [
            remote(ez.at[step(u, k), part], r1e.at[k - 1, part], e1s.at[k - 1, e], e1r.at[k - 1, e], to_u(k))
            for k in range(1, 4)
        ]

    def early2(q):
        e = q - EARLY
        part = pl.ds(2 * e, 2)
        return [
            remote(s1e.at[step(v, k), part], r2e.at[k - 1, part], e2s.at[k - 1, e], e2r.at[k - 1, e], to_v(k))
            for k in range(1, 4)
        ]

    def early_sum1(q):
        for e in (2 * (q - EARLY), 2 * (q - EARLY) + 1):
            total = ez[u, e].astype(F32)
            for k in range(3):
                total = total + r1e[k, e].astype(F32)
            for j in range(4):
                s1e[j, e] = total[:, 256 * j : 256 * j + 256]

    def early_sum2(q):
        for source in range(2):
            e = 2 * (q - EARLY) + source
            total = s1e[v, e]
            for k in range(3):
                total = total + r2e[k, e]
            slot = 2 * lax.rem(z + 8 - OFFSETS[q], 8) + source
            gbuf[slot, v, 0], gbuf[slot, v, 1] = split(total)

    def pair(q):
        return pl.ds(2 * lax.rem(z + 8 - OFFSETS[q], 8), 2)

    class Gather:
        def __init__(self, piece, half, me, to, ssem, rsem, passing):
            own_piece = piece(me)
            self.direct = [
                remote(own_piece, own_piece, ssem.at[0], rsem.at[0], to(1)),
                remote(own_piece, own_piece, ssem.at[1], rsem.at[1], to(3)),
            ]
            if passing:
                after, before = half(step(me, 3), 0), half(step(me, 1), 1)
                self.passed = [
                    remote(after, after, ssem.at[2], rsem.at[2], to(1)),
                    remote(before, before, ssem.at[3], rsem.at[3], to(3)),
                ]
            else:
                self.passed = [remote(own_piece, own_piece, ssem.at[2], rsem.at[2], to(2))]
            self.passing = passing

        def start(self):
            start_all(self.direct)
            if not self.passing:
                start_all(self.passed)

        def go_on(self):
            if self.passing:
                for received, onward in zip(self.direct, self.passed):
                    received.wait_recv()
                    start_all([onward])

        def wait(self):
            if not self.passing:
                recv_all(self.direct)
            recv_all(self.passed)

        def sent(self):
            send_all(self.direct)
            send_all(self.passed)

    def gather1(q):
        return Gather(
            lambda i: gbuf.at[pair(q), i], lambda i, h: gbuf.at[pair(q), i, h], v, to_v, g1s.at[q], g1r.at[q], PASS1[q]
        )

    def gather2(q):
        return Gather(
            lambda i: hbuf.at[:, pair(q), i], lambda i, h: hbuf.at[h, pair(q), i], u, to_u, g2s.at[q], g2r.at[q], PASS2[q]
        )

    def times_right(qs):
        rows = 32 * len(qs)
        total = None
        for j in range(4):
            cols = slice(256 * j, 256 * j + 256)
            high, low = (
                jnp.concatenate([gbuf[pair(i), j, h].reshape(32, 256) for i in qs], axis=0) for h in range(2)
            )
            b_high = rg[:, 0, :, cols].reshape(256, 256)
            b_low = rg[:, 1, :, cols].reshape(256, 256)
            both = dot(jnp.concatenate([high, low], axis=0), b_high, NT)
            part = both[:rows] + both[rows:] + dot(high, b_low, NT)
            total = part if total is None else total + part
        high, low = split(total)
        for i, q in enumerate(qs):
            hbuf[0, pair(q), u] = high[32 * i : 32 * i + 32].reshape(2, 16, 256)
            hbuf[1, pair(q), u] = low[32 * i : 32 * i + 32].reshape(2, 16, 256)

    def left_times(part):
        high, low = [], []
        for q in part:
            cols = pl.ds(pl.multiple_of(128 * lax.rem(z + 8 - OFFSETS[q], 8), 128), 128)
            high.append(lg[:, 0, :, cols].reshape(256, 128))
            low.append(lg[:, 1, :, cols].reshape(256, 128))
        a_high, a_low = (jnp.concatenate(cols, axis=1) for cols in (high, low))
        b_high, b_low = (
            jnp.concatenate([hbuf[h, pair(q)].reshape(128, 256) for q in part], axis=0) for h in range(2)
        )
        return dot(a_high, b_high, NN) + dot(a_high, b_low, NN) + dot(a_low, b_high, NN)

    rights = Gather(lambda i: rg.at[i], lambda i, h: rg.at[i, h], u, to_u, rs, rrc, PASSR)
    lefts = Gather(lambda i: lg.at[i], lambda i, h: lg.at[i, h], v, to_v, ls, lrc, PASSL)

    def slots(c):
        return range(PARTS[c][0], PARTS[c][0] + PARTS[c][1])

    load_g.wait()
    for c in range(CHUNKS):
        for q in slots(c):
            stage(q)
        if c == 0:
            pl.semaphore_wait(barrier, 21)
        start_all(stage1(c))
        if c == 0:
            for q in slots(CHUNKS):
                stage(q)
                send_early(q)

    load_r.wait()
    rg[u, 0], rg[u, 1] = split(rv[...])
    load_l.wait()
    lg[v, 0], lg[v, 1] = split(lv[...])

    def sum_first(c):
        recv_all(stage1(c))
        for q in slots(c):
            sum1(q)
        start_all(stage2(c))

    def sum_second(c):
        recv_all(stage2(c))
        for q in slots(c):
            sum2(q)
            send_z(q)

    def spread_rows(c):
        for q in slots(c):
            if c < CHUNKS:
                wait_z(q)
            else:
                recv_all(early2(q))
                early_sum2(q)
            gather1(q).start()

    def early_first():
        for q in slots(CHUNKS):
            wait_early(q)
            start_all(early1(q))

    def early_second():
        for q in slots(CHUNKS):
            recv_all(early1(q))
            early_sum1(q)
            start_all(early2(q))

    def pass_rows(c):
        for q in slots(c):
            gather1(q).go_on()

    def multiply_right(c):
        for q in slots(c):
            gather1(q).wait()
        times_right(slots(c))
        for q in slots(c):
            gather2(q).start()

    def pass_products(c):
        for q in slots(c):
            gather2(q).go_on()

    def multiply_left(c):
        for q in slots(c):
            gather2(q).wait()
        product = left_times(slots(c)).reshape(4, 64, 256)
        pt[...] = product if c == 0 else pt[...] + product

    def norm_of_gradient():
        tile = gbuf[:, v]
        tile = (tile[:, 0].astype(F32) + tile[:, 1].astype(F32)).reshape(256, 256)
        scx[x, 0] = fold(tile * tile)

    sum_first(0)
    early_first()
    sum_first(1)
    sum_first(2)
    sum_second(0)
    rights.start()
    sum_second(2)
    sum_second(1)
    early_second()
    rights.go_on()
    lefts.start()
    spread_rows(0)
    spread_rows(1)
    spread_rows(2)
    spread_rows(3)
    pass_rows(0)
    pass_rows(1)
    pass_rows(2)
    pass_rows(3)
    norm_of_gradient()
    lefts.go_on()
    rights.wait()
    multiply_right(0)
    multiply_right(1)
    multiply_right(2)
    multiply_right(3)
    pass_products(0)
    pass_products(1)
    pass_products(2)
    lefts.wait()
    multiply_left(0)
    pass_products(3)
    multiply_left(1)
    multiply_left(3)
    multiply_left(2)

    tile = pt[...].reshape(256, 256)
    scx[x, 1] = fold(tile * tile)

    norms_x = [remote(scx.at[x], scx.at[x], cxs.at[k - 1], cxr.at[k - 1], to_x(k)) for k in range(1, 4)]
    norms_y = [remote(scy.at[y], scy.at[y], cys.at[k - 1], cyr.at[k - 1], to_y(k)) for k in range(1, 4)]
    turn = [remote(pt.at[step(v, k)], pr.at[v], ts.at[k - 1], tr.at[k - 1], to_v(k)) for k in range(1, 4)]
    start_all(norms_x)
    start_all(turn)
    pr[v] = pt[v]
    load_m.wait()
    for c in range(CHUNKS):
        send_all(stage1(c))
    recv_all(norms_x)
    scy[y] = scx[0] + scx[1] + scx[2] + scx[3]
    start_all(norms_y)
    for c in range(CHUNKS):
        send_all(stage2(c))
    for q in range(EARLY):
        sent_z(q)
    for q in slots(CHUNKS):
        sent_early(q)
        send_all(early1(q))
        send_all(early2(q))
    recv_all(turn)
    recv_all(norms_y)
    sums = scy[0] + scy[1] + scy[2] + scy[3]
    entries = 1024 * 1024
    grad_total = jnp.sum(sums[0], keepdims=True)
    prec_total = jnp.sum(sums[1], keepdims=True)
    scale = jnp.sqrt(grad_total / entries + epsilon) / jnp.sqrt(prec_total / entries + epsilon)

    def update(columns):
        for j in range(8):
            cols = slice(128 * j, 128 * j + 128)
            graft = columns(j) * scale
            moved = decay_rate * mv[:, cols] + graft
            nm_o[0, :, cols] = moved
            h32[:, cols] = decay_rate * moved + graft

    @pl.when(core == 0)
    def _():
        update(lambda j: pr[j // 2, :, 128 * (j % 2) : 128 * (j % 2) + 128])

    @pl.when(core == 1)
    def _():
        def columns(j):
            strip = slice(64 * (j // 2), 64 * (j // 2) + 64)
            first = 2 * (j % 2)
            return jnp.concatenate([pr[first, :, strip], pr[first + 1, :, strip]], axis=1)

        update(columns)

    hb[...] = h32[...].reshape(16, 4, 1024).astype(BF)

    def back(k):
        to = lax.rem(shard + k, 16)
        return remote(hb.at[to], fin.at[shard], fs.at[k], fr.at[k], {"shard": to})

    order = (8, 9, 7, 10, 6, 11, 5, 12, 4, 13, 3, 14, 2, 15, 1)
    for k in order:
        back(k).start()
    fin[shard] = hb[shard]
    send_all(norms_x)
    send_all(norms_y)
    send_all(turn)
    rights.sent()
    lefts.sent()
    for q in range(8):
        gather1(q).sent()
        gather2(q).sent()
    for k in order:
        back(k).wait_recv()
    for b in range(16):
        dir_o[b] = fin[own[b]]
    for k in order:
        back(k).wait_send()


def last(d_in, m_in, d_out, m_out, sem):
    copies = [pltpu.make_async_copy(m_in, m_out, sem.at[0]), pltpu.make_async_copy(d_in, d_out, sem.at[1])]
    for copy in copies:
        copy.start()
    for copy in copies:
        copy.wait()


def body(grad_partial, owner_slots, left_roots, right_roots, momentum):
    dma = pltpu.SemaphoreType.DMA
    any_space = pl.BlockSpec(memory_space=pl.ANY)
    direction, new_momentum = pl.pallas_call(
        kernel,
        out_shape=(
            jax.ShapeDtypeStruct((16, 4, 1024), BF),
            jax.ShapeDtypeStruct((1, 64, 1024), F32),
        ),
        in_specs=[any_space, pl.BlockSpec(memory_space=pltpu.SMEM), any_space, any_space, any_space],
        out_specs=(pl.BlockSpec(memory_space=pltpu.VMEM),) * 2,
        scratch_shapes=[
            pltpu.VMEM((16, 64, 1024), BF),
            pltpu.VMEM((64, 1024), F32),
            pltpu.VMEM((64, 1024), F32),
            pltpu.VMEM((64, 1024), F32),
            pltpu.VMEM((4, 8, 16, 1024), BF),
            pltpu.VMEM((4, 8, 16, 1024), BF),
            pltpu.VMEM((3, 8, 16, 1024), BF),
            pltpu.VMEM((3, 8, 16, 1024), BF),
            pltpu.VMEM((4, 8, 16, 256), F32),
            pltpu.VMEM((4, 8, 16, 256), F32),
            pltpu.VMEM((3, 8, 16, 256), F32),
            pltpu.VMEM((3, 8, 16, 256), F32),
            pltpu.VMEM((4, 6, 16, 1024), BF),
            pltpu.VMEM((3, 6, 16, 1024), BF),
            pltpu.VMEM((4, 6, 16, 256), F32),
            pltpu.VMEM((3, 6, 16, 256), F32),
            pltpu.VMEM((2, 8, 2, 16, 256), BF),
            pltpu.VMEM((16, 4, 2, 16, 256), BF),
            pltpu.VMEM((2, 16, 4, 16, 256), BF),
            pltpu.VMEM((4, 2, 64, 1024), BF),
            pltpu.VMEM((4, 2, 64, 1024), BF),
            pltpu.VMEM((4, 64, 256), F32),
            pltpu.VMEM((4, 64, 256), F32),
            pltpu.VMEM((4, 2, 8, 128), F32),
            pltpu.VMEM((4, 2, 8, 128), F32),
            pltpu.VMEM((64, 1024), F32),
            pltpu.VMEM((16, 4, 1024), BF),
            pltpu.VMEM((16, 4, 1024), BF),
            pltpu.VMEM((16, 4, 1024), BF),
            pltpu.VMEM((64, 1024), F32),
            dma((6,)),
            dma((2, 3)), dma((3, 2)),
            dma((3, 3)), dma((3, 3)), dma((3, 3)), dma((3, 3)),
            dma((3, CHUNKS, 2)), dma((3, CHUNKS, 2)),
            dma((3, CHUNKS, 2)), dma((3, CHUNKS, 2)),
            dma((2, 8)), dma((8, 2)),
            dma((4,)), dma((4,)), dma((4,)), dma((4,)),
            dma((8, 4)), dma((8, 4)), dma((8, 4)), dma((8, 4)),
            dma((3,)), dma((3,)),
            dma((3,)), dma((3,)), dma((3,)), dma((3,)),
            dma((16,)), dma((16,)),
        ],
        compiler_params=pltpu.CompilerParams(
            collective_id=0, has_side_effects=True, vmem_limit_bytes=54800 * 1024
        ),
    )(grad_partial, owner_slots, jnp.swapaxes(left_roots, 1, 2), right_roots, momentum)
    vmem = pl.BlockSpec(memory_space=pltpu.VMEM)
    return pl.pallas_call(
        last,
        out_shape=(
            jax.ShapeDtypeStruct((16, 4, 1024), BF),
            jax.ShapeDtypeStruct((1, 64, 1024), F32),
        ),
        in_specs=[vmem, vmem],
        out_specs=(any_space, any_space),
        scratch_shapes=[dma((2,))],
        compiler_params=pltpu.CompilerParams(vmem_limit_bytes=2 * 2**20),
    )(direction, new_momentum)


def solution(mesh):
    return jax.shard_map(
        body,
        mesh=mesh,
        in_specs=(
            P("dp", None, "shard", None),
            P(),
            P("shard", None, "dp"),
            P("shard", "dp", None),
            P("shard", "dp", None),
        ),
        out_specs=(P(None, ("dp", "shard"), None), P("shard", "dp", None)),
        check_vma=False,
    )
```

```python
import jax
import jax.numpy as jnp
from jax import lax
from jax.experimental import pallas as pl
from jax.experimental.pallas import tpu as pltpu
from jax.sharding import PartitionSpec as P

epsilon = 1e-06
decay_rate = 0.9

MESH = pl.DeviceIdType.MESH
BF = jnp.bfloat16
F32 = jnp.float32
PARTS = ((0, 2), (2, 2), (4, 1), (5, 3))
EARLY = 5
CHUNKS = len(PARTS) - 1
OFFSETS = (4, 3, 5, 2, 6, 1, 7, 0)
PASS1 = (True,) * 5 + (False,) * 3
PASS2 = (True,) * 5 + (False,) * 3
PASSR = True
PASSL = True
NT = (((1,), (1,)), ((), ()))
NN = (((1,), (0,)), ((), ()))


def split(value):
    high = value.astype(BF)
    return high, (value - high.astype(F32)).astype(BF)


def dot(a, b, dims):
    return lax.dot_general(a, b, dims, preferred_element_type=F32)


def fold(value):
    rows = value.reshape(32, 8, 256).sum(axis=0)
    return rows[:, :128] + rows[:, 128:]


def kernel(
    gp, own, lr, rr, mo, dir_o, nm_o,
    gv, lv, rv, mv, stx, sty, r1x, r1y, s1x, s1y, r2x, r2y, ez, r1e, s1e, r2e, zt, gbuf, hbuf, lg, rg,
    pt, pr, scx, h32, hb, fin, ob, nm,
    loc, known, es, er, e1s, e1r, e2s, e2r, s1s, s1r, s2s, s2r, zs, zr, ls, lrc, rs, rrc, g1s, g1r, g2s, g2r, ts, tr,
    cxs, cxr, fs, fr,
):
    dp = lax.axis_index("dp")
    shard = lax.axis_index("shard")
    x, y = lax.rem(dp, 4), lax.div(dp, 4)
    z, core = lax.div(shard, 2), lax.rem(shard, 2)
    u = (1 - core) * x + core * y
    v = (1 - core) * y + core * x

    def step(i, k):
        return lax.rem(i + k, 4)

    def to_x(k):
        return {"dp": y * 4 + step(x, k)}

    def to_y(k):
        return {"dp": step(y, k) * 4 + x}

    def to_dp(k):
        return {"dp": step(y, k // 4) * 4 + step(x, k % 4)}

    def to_u(k):
        return {"dp": (1 - core) * (y * 4 + step(x, k)) + core * (step(y, k) * 4 + x)}

    def to_v(k):
        return {"dp": core * (y * 4 + step(x, k)) + (1 - core) * (step(y, k) * 4 + x)}

    def remote(src, dst, ssem, rsem, device):
        return pltpu.make_async_remote_copy(
            src_ref=src, dst_ref=dst, send_sem=ssem, recv_sem=rsem, device_id=device, device_id_type=MESH
        )

    def start_all(copies):
        for copy in copies:
            copy.start()

    def recv_all(copies):
        for copy in copies:
            copy.wait_recv()

    def send_all(copies):
        for copy in copies:
            copy.wait_send()

    load_g = pltpu.make_async_copy(gp.at[0], gv, loc.at[0])
    load_l = pltpu.make_async_copy(lr.at[0], lv, loc.at[1])
    load_r = pltpu.make_async_copy(rr.at[0], rv, loc.at[2])
    load_m = pltpu.make_async_copy(mo.at[0], mv, loc.at[3])
    load_g.start()
    load_r.start()
    load_l.start()
    load_m.start()

    barrier = pltpu.get_barrier_semaphore()
    for k in range(1, 16):
        pl.semaphore_signal(barrier, inc=1, device_id=to_dp(k), device_id_type=MESH)

    def along_z(k):
        return {"shard": lax.rem(z + k + 8, 8) * 2 + core}

    other_core = {"shard": z * 2 + 1 - core}
    cross = ({"shard": lax.rem(z + 1, 8) * 2 + 1 - core}, {"shard": lax.rem(z + 7, 8) * 2 + 1 - core})
    near = (along_z(1), along_z(-1), other_core)
    for device in near + cross:
        pl.semaphore_signal(barrier, inc=1, device_id=device, device_id_type=MESH)

    rounds = (near, (along_z(2), along_z(-2)), (other_core,))

    def tell(i):
        for device in rounds[i]:
            pl.semaphore_signal(known.at[i], inc=1, device_id=device, device_id_type=MESH)

    def hear(i):
        pl.semaphore_wait(known.at[i], len(rounds[i]))

    def block_of(slot):
        found = jnp.int32(0)
        for b in range(16):
            found = jnp.where(own[b] == slot, b, found)
        return found

    def stage(q):
        zq = lax.rem(z + OFFSETS[q], 8)
        for target, staged in enumerate((stx, sty)):
            block = gv[block_of(zq * 2 + target)]
            for i in range(4):
                staged[i, q] = block[16 * i : 16 * i + 16]

    def stage1(c):
        part = pl.ds(*PARTS[c])
        out = []
        for k in range(1, 4):
            out.append(remote(stx.at[step(x, k), part], r1x.at[k - 1, part], s1s.at[k - 1, c, 0], s1r.at[k - 1, c, 0], to_x(k)))
            out.append(remote(sty.at[step(y, k), part], r1y.at[k - 1, part], s1s.at[k - 1, c, 1], s1r.at[k - 1, c, 1], to_y(k)))
        return out

    def sum1(q):
        for staged, got, summed, me in ((stx, r1x, s1x, x), (sty, r1y, s1y, y)):
            total = staged[me, q].astype(F32)
            for k in range(3):
                total = total + got[k, q].astype(F32)
            for j in range(4):
                summed[j, q] = total[:, 256 * j : 256 * j + 256]

    def stage2(c):
        part = pl.ds(*PARTS[c])
        out = []
        for k in range(1, 4):
            out.append(remote(s1x.at[step(y, k), part], r2x.at[k - 1, part], s2s.at[k - 1, c, 0], s2r.at[k - 1, c, 0], to_y(k)))
            out.append(remote(s1y.at[step(x, k), part], r2y.at[k - 1, part], s2s.at[k - 1, c, 1], s2r.at[k - 1, c, 1], to_x(k)))
        return out

    def sum2(q):
        for target, (summed, got, me) in enumerate(((s1x, r2x, y), (s1y, r2y, x))):
            total = summed[me, q]
            for k in range(3):
                total = total + got[k, q]
            zt[target, q, 0], zt[target, q, 1] = split(total)

    def exchange(q, target):
        dst = gbuf.at[shard, y if target == 0 else x]
        device = {"shard": lax.rem(z + OFFSETS[q], 8) * 2 + target}
        return remote(zt.at[target, q], dst, zs.at[target, q], zr.at[q, core], device)

    def send_z(q):
        if OFFSETS[q]:
            exchange(q, 0).start()
            exchange(q, 1).start()
        else:
            @pl.when(core == 0)
            def _():
                exchange(q, 1).start()
                gbuf[shard, y] = zt[0, q]

            @pl.when(core == 1)
            def _():
                exchange(q, 0).start()
                gbuf[shard, x] = zt[1, q]

    def wait_z(q):
        for source in range(2):
            def wait():
                remote(zt.at[0, q], gbuf.at[shard, v], zs.at[0, q], zr.at[q, source], {"shard": shard}).wait_recv()

            if OFFSETS[q]:
                wait()
            else:
                pl.when(core != source)(wait)

    def sent_z(q):
        if OFFSETS[q]:
            exchange(q, 0).wait_send()
            exchange(q, 1).wait_send()
        else:
            pl.when(core == 0)(lambda: exchange(q, 1).wait_send())
            pl.when(core == 1)(lambda: exchange(q, 0).wait_send())

    def early(q, target):
        staged = (stx, sty)[target]
        e = q - EARLY
        device = {"shard": lax.rem(z + OFFSETS[q], 8) * 2 + target}
        return remote(staged.at[:, q], ez.at[:, 2 * e + core], es.at[target, e], er.at[e, core], device)

    def send_early(q):
        if OFFSETS[q]:
            early(q, 0).start()
            early(q, 1).start()
        else:
            @pl.when(core == 0)
            def _():
                early(q, 1).start()
                ez[:, 2 * (q - EARLY)] = stx[:, q]

            @pl.when(core == 1)
            def _():
                early(q, 0).start()
                ez[:, 2 * (q - EARLY) + 1] = sty[:, q]

    def wait_early(q):
        e = q - EARLY
        for source in range(2):
            def wait():
                remote(stx.at[:, q], ez.at[:, 2 * e + source], es.at[0, e], er.at[e, source], {"shard": shard}).wait_recv()

            if OFFSETS[q]:
                wait()
            else:
                pl.when(core != source)(wait)

    def sent_early(q):
        if OFFSETS[q]:
            early(q, 0).wait_send()
            early(q, 1).wait_send()
        else:
            pl.when(core == 0)(lambda: early(q, 1).wait_send())
            pl.when(core == 1)(lambda: early(q, 0).wait_send())

    def early1(q):
        e = q - EARLY
        part = pl.ds(2 * e, 2)
        return [
            remote(ez.at[step(u, k), part], r1e.at[k - 1, part], e1s.at[k - 1, e], e1r.at[k - 1, e], to_u(k))
            for k in range(1, 4)
        ]

    def early2(q):
        e = q - EARLY
        part = pl.ds(2 * e, 2)
        return [
            remote(s1e.at[step(v, k), part], r2e.at[k - 1, part], e2s.at[k - 1, e], e2r.at[k - 1, e], to_v(k))
            for k in range(1, 4)
        ]

    def early_sum1(q):
        for e in (2 * (q - EARLY), 2 * (q - EARLY) + 1):
            total = ez[u, e].astype(F32)
            for k in range(3):
                total = total + r1e[k, e].astype(F32)
            for j in range(4):
                s1e[j, e] = total[:, 256 * j : 256 * j + 256]

    def early_sum2(q):
        for source in range(2):
            e = 2 * (q - EARLY) + source
            total = s1e[v, e]
            for k in range(3):
                total = total + r2e[k, e]
            slot = 2 * lax.rem(z + 8 - OFFSETS[q], 8) + source
            gbuf[slot, v, 0], gbuf[slot, v, 1] = split(total)

    def pair(q):
        return pl.ds(2 * lax.rem(z + 8 - OFFSETS[q], 8), 2)

    class Gather:
        def __init__(self, piece, half, me, to, ssem, rsem, passing):
            own_piece = piece(me)
            self.direct = [
                remote(own_piece, own_piece, ssem.at[0], rsem.at[0], to(1)),
                remote(own_piece, own_piece, ssem.at[1], rsem.at[1], to(3)),
            ]
            if passing:
                after, before = half(step(me, 3), 0), half(step(me, 1), 1)
                self.passed = [
                    remote(after, after, ssem.at[2], rsem.at[2], to(1)),
                    remote(before, before, ssem.at[3], rsem.at[3], to(3)),
                ]
            else:
                self.passed = [remote(own_piece, own_piece, ssem.at[2], rsem.at[2], to(2))]
            self.passing = passing

        def start(self):
            start_all(self.direct)
            if not self.passing:
                start_all(self.passed)

        def go_on(self):
            if self.passing:
                for received, onward in zip(self.direct, self.passed):
                    received.wait_recv()
                    start_all([onward])

        def wait(self):
            if not self.passing:
                recv_all(self.direct)
            recv_all(self.passed)

        def sent(self):
            send_all(self.direct)
            send_all(self.passed)

    def gather1(q):
        return Gather(
            lambda i: gbuf.at[pair(q), i], lambda i, h: gbuf.at[pair(q), i, h], v, to_v, g1s.at[q], g1r.at[q], PASS1[q]
        )

    def gather2(q):
        return Gather(
            lambda i: hbuf.at[:, pair(q), i], lambda i, h: hbuf.at[h, pair(q), i], u, to_u, g2s.at[q], g2r.at[q], PASS2[q]
        )

    def times_right(qs):
        rows = 32 * len(qs)
        total = None
        for j in range(4):
            cols = slice(256 * j, 256 * j + 256)
            high, low = (
                jnp.concatenate([gbuf[pair(i), j, h].reshape(32, 256) for i in qs], axis=0) for h in range(2)
            )
            b_high = rg[:, 0, :, cols].reshape(256, 256)
            b_low = rg[:, 1, :, cols].reshape(256, 256)
            both = dot(jnp.concatenate([high, low], axis=0), b_high, NT)
            part = both[:rows] + both[rows:] + dot(high, b_low, NT)
            total = part if total is None else total + part
        high, low = split(total)
        for i, q in enumerate(qs):
            hbuf[0, pair(q), u] = high[32 * i : 32 * i + 32].reshape(2, 16, 256)
            hbuf[1, pair(q), u] = low[32 * i : 32 * i + 32].reshape(2, 16, 256)

    def left_times(part):
        high, low = [], []
        for q in part:
            cols = pl.ds(pl.multiple_of(128 * lax.rem(z + 8 - OFFSETS[q], 8), 128), 128)
            high.append(lg[:, 0, :, cols].reshape(256, 128))
            low.append(lg[:, 1, :, cols].reshape(256, 128))
        a_high, a_low = (jnp.concatenate(cols, axis=1) for cols in (high, low))
        b_high, b_low = (
            jnp.concatenate([hbuf[h, pair(q)].reshape(128, 256) for q in part], axis=0) for h in range(2)
        )
        return dot(a_high, b_high, NN) + dot(a_high, b_low, NN) + dot(a_low, b_high, NN)

    rights = Gather(lambda i: rg.at[i], lambda i, h: rg.at[i, h], u, to_u, rs, rrc, PASSR)
    lefts = Gather(lambda i: lg.at[i], lambda i, h: lg.at[i, h], v, to_v, ls, lrc, PASSL)

    def slots(c):
        return range(PARTS[c][0], PARTS[c][0] + PARTS[c][1])

    load_g.wait()
    for c in range(CHUNKS):
        for q in slots(c):
            stage(q)
        if c == 0:
            pl.semaphore_wait(barrier, 20)
        start_all(stage1(c))
        if c == 0:
            tell(0)
            for q in slots(CHUNKS):
                stage(q)
                send_early(q)

    load_r.wait()
    rg[u, 0], rg[u, 1] = split(rv[...])
    load_l.wait()
    lg[v, 0], lg[v, 1] = split(lv[...])

    def sum_first(c):
        recv_all(stage1(c))
        for q in slots(c):
            sum1(q)
        start_all(stage2(c))

    def sum_second(c):
        recv_all(stage2(c))
        for q in slots(c):
            sum2(q)
            send_z(q)

    def spread_rows(c):
        for q in slots(c):
            if c < CHUNKS:
                wait_z(q)
            else:
                recv_all(early2(q))
                early_sum2(q)
            gather1(q).start()

    def early_first():
        for q in slots(CHUNKS):
            wait_early(q)
            start_all(early1(q))

    def early_second():
        for q in slots(CHUNKS):
            recv_all(early1(q))
            early_sum1(q)
            start_all(early2(q))

    def pass_rows(c):
        for q in slots(c):
            gather1(q).go_on()

    def multiply_right(c):
        for q in slots(c):
            gather1(q).wait()
        times_right(slots(c))
        for q in slots(c):
            gather2(q).start()

    def pass_products(c):
        for q in slots(c):
            gather2(q).go_on()

    def multiply_left(c):
        for q in slots(c):
            gather2(q).wait()
        product = left_times(slots(c)).reshape(4, 64, 256)
        pt[...] = product if c == 0 else pt[...] + product

    def norms(kind):
        part = scx.at[kind, dp]
        return [
            remote(part, part, cxs.at[kind, k], cxr.at[kind, k], to_dp(k))
            for k in (10, 6, 14, 9, 11, 5, 7, 13, 15, 2, 8, 1, 3, 4, 12)
        ]

    def norm_of_gradient():
        tile = gbuf[:, v]
        tile = (tile[:, 0].astype(F32) + tile[:, 1].astype(F32)).reshape(256, 256)
        scx[0, dp] = fold(tile * tile)
        start_all(norms(0))

    sum_first(0)
    hear(0)
    tell(1)
    early_first()
    hear(1)
    tell(2)
    sum_first(1)
    sum_first(2)
    hear(2)
    sum_second(0)
    rights.start()
    sum_second(2)
    sum_second(1)
    early_second()
    rights.go_on()
    lefts.start()
    spread_rows(0)
    spread_rows(1)
    spread_rows(2)
    spread_rows(3)
    pass_rows(0)
    pass_rows(1)
    pass_rows(2)
    pass_rows(3)
    norm_of_gradient()
    lefts.go_on()
    rights.wait()
    multiply_right(0)
    multiply_right(1)
    multiply_right(2)
    multiply_right(3)
    pass_products(0)
    pass_products(1)
    pass_products(2)
    lefts.wait()
    multiply_left(0)
    pass_products(3)
    multiply_left(1)
    multiply_left(3)
    multiply_left(2)

    tile = pt[...].reshape(256, 256)
    scx[1, dp] = fold(tile * tile)

    turn = [remote(pt.at[step(v, k)], pr.at[v], ts.at[k - 1], tr.at[k - 1], to_v(k)) for k in range(1, 4)]
    start_all(norms(1))
    start_all(turn)
    pr[v] = pt[v]
    load_m.wait()
    for c in range(CHUNKS):
        send_all(stage1(c))
    for c in range(CHUNKS):
        send_all(stage2(c))
    for q in range(EARLY):
        sent_z(q)
    for q in slots(CHUNKS):
        sent_early(q)
        send_all(early1(q))
        send_all(early2(q))
    recv_all(turn)
    recv_all(norms(0))
    recv_all(norms(1))
    entries = 1024 * 1024
    grad_total = jnp.sum(scx[0].sum(axis=0), keepdims=True)
    prec_total = jnp.sum(scx[1].sum(axis=0), keepdims=True)
    scale = jnp.sqrt(grad_total / entries + epsilon) / jnp.sqrt(prec_total / entries + epsilon)

    def update(columns):
        for j in range(8):
            cols = slice(128 * j, 128 * j + 128)
            graft = columns(j) * scale
            moved = decay_rate * mv[:, cols] + graft
            nm_o[0, :, cols] = moved
            h32[:, cols] = decay_rate * moved + graft

    @pl.when(core == 0)
    def _():
        update(lambda j: pr[j // 2, :, 128 * (j % 2) : 128 * (j % 2) + 128])

    @pl.when(core == 1)
    def _():
        def columns(j):
            strip = slice(64 * (j // 2), 64 * (j // 2) + 64)
            first = 2 * (j % 2)
            return jnp.concatenate([pr[first, :, strip], pr[first + 1, :, strip]], axis=1)

        update(columns)

    hb[...] = h32[...].reshape(16, 4, 1024).astype(BF)

    def back(k):
        to = lax.rem(shard + k, 16)
        return remote(hb.at[to], fin.at[shard], fs.at[k], fr.at[k], {"shard": to})

    order = (8, 9, 7, 10, 6, 11, 5, 12, 4, 13, 3, 14, 2, 15, 1)
    for k in order:
        back(k).start()
    fin[shard] = hb[shard]
    send_all(norms(0))
    send_all(norms(1))
    send_all(turn)
    rights.sent()
    lefts.sent()
    for q in range(8):
        gather1(q).sent()
        gather2(q).sent()
    for k in order:
        back(k).wait_recv()
    for b in range(16):
        dir_o[b] = fin[own[b]]
    for k in order:
        back(k).wait_send()


def last(d_in, m_in, d_out, m_out, sem):
    copies = [pltpu.make_async_copy(m_in, m_out, sem.at[0]), pltpu.make_async_copy(d_in, d_out, sem.at[1])]
    for copy in copies:
        copy.start()
    for copy in copies:
        copy.wait()


def body(grad_partial, owner_slots, left_roots, right_roots, momentum):
    dma = pltpu.SemaphoreType.DMA
    any_space = pl.BlockSpec(memory_space=pl.ANY)
    direction, new_momentum = pl.pallas_call(
        kernel,
        out_shape=(
            jax.ShapeDtypeStruct((16, 4, 1024), BF),
            jax.ShapeDtypeStruct((1, 64, 1024), F32),
        ),
        in_specs=[any_space, pl.BlockSpec(memory_space=pltpu.SMEM), any_space, any_space, any_space],
        out_specs=(pl.BlockSpec(memory_space=pltpu.VMEM),) * 2,
        scratch_shapes=[
            pltpu.VMEM((16, 64, 1024), BF),
            pltpu.VMEM((64, 1024), F32),
            pltpu.VMEM((64, 1024), F32),
            pltpu.VMEM((64, 1024), F32),
            pltpu.VMEM((4, 8, 16, 1024), BF),
            pltpu.VMEM((4, 8, 16, 1024), BF),
            pltpu.VMEM((3, 8, 16, 1024), BF),
            pltpu.VMEM((3, 8, 16, 1024), BF),
            pltpu.VMEM((4, 8, 16, 256), F32),
            pltpu.VMEM((4, 8, 16, 256), F32),
            pltpu.VMEM((3, 8, 16, 256), F32),
            pltpu.VMEM((3, 8, 16, 256), F32),
            pltpu.VMEM((4, 6, 16, 1024), BF),
            pltpu.VMEM((3, 6, 16, 1024), BF),
            pltpu.VMEM((4, 6, 16, 256), F32),
            pltpu.VMEM((3, 6, 16, 256), F32),
            pltpu.VMEM((2, 8, 2, 16, 256), BF),
            pltpu.VMEM((16, 4, 2, 16, 256), BF),
            pltpu.VMEM((2, 16, 4, 16, 256), BF),
            pltpu.VMEM((4, 2, 64, 1024), BF),
            pltpu.VMEM((4, 2, 64, 1024), BF),
            pltpu.VMEM((4, 64, 256), F32),
            pltpu.VMEM((4, 64, 256), F32),
            pltpu.VMEM((2, 16, 8, 128), F32),
            pltpu.VMEM((64, 1024), F32),
            pltpu.VMEM((16, 4, 1024), BF),
            pltpu.VMEM((16, 4, 1024), BF),
            pltpu.VMEM((16, 4, 1024), BF),
            pltpu.VMEM((64, 1024), F32),
            dma((6,)),
            pltpu.SemaphoreType.REGULAR((3,)),
            dma((2, 3)), dma((3, 2)),
            dma((3, 3)), dma((3, 3)), dma((3, 3)), dma((3, 3)),
            dma((3, CHUNKS, 2)), dma((3, CHUNKS, 2)),
            dma((3, CHUNKS, 2)), dma((3, CHUNKS, 2)),
            dma((2, 8)), dma((8, 2)),
            dma((4,)), dma((4,)), dma((4,)), dma((4,)),
            dma((8, 4)), dma((8, 4)), dma((8, 4)), dma((8, 4)),
            dma((3,)), dma((3,)),
            dma((2, 16)), dma((2, 16)),
            dma((16,)), dma((16,)),
        ],
        compiler_params=pltpu.CompilerParams(
            collective_id=0, has_side_effects=True, vmem_limit_bytes=54800 * 1024
        ),
    )(grad_partial, owner_slots, jnp.swapaxes(left_roots, 1, 2), right_roots, momentum)
    vmem = pl.BlockSpec(memory_space=pltpu.VMEM)
    return pl.pallas_call(
        last,
        out_shape=(
            jax.ShapeDtypeStruct((16, 4, 1024), BF),
            jax.ShapeDtypeStruct((1, 64, 1024), F32),
        ),
        in_specs=[vmem, vmem],
        out_specs=(any_space, any_space),
        scratch_shapes=[dma((2,))],
        compiler_params=pltpu.CompilerParams(vmem_limit_bytes=2 * 2**20),
    )(direction, new_momentum)


def solution(mesh):
    return jax.shard_map(
        body,
        mesh=mesh,
        in_specs=(
            P("dp", None, "shard", None),
            P(),
            P("shard", None, "dp"),
            P("shard", "dp", None),
            P("shard", "dp", None),
        ),
        out_specs=(P(None, ("dp", "shard"), None), P("shard", "dp", None)),
        check_vma=False,
    )
```

```python
import jax
import jax.numpy as jnp
from jax import lax
from jax.experimental import pallas as pl
from jax.experimental.pallas import tpu as pltpu
from jax.sharding import PartitionSpec as P

epsilon = 1e-06
decay_rate = 0.9

MESH = pl.DeviceIdType.MESH
BF = jnp.bfloat16
F32 = jnp.float32
PARTS = ((0, 2), (2, 2), (4, 1), (5, 3))
EARLY = 5
CHUNKS = len(PARTS) - 1
OFFSETS = (4, 3, 5, 2, 6, 1, 7, 0)
PASS1 = (True,) * 5 + (False,) * 3
PASS2 = (True,) * 5 + (False,) * 3
PASSR = True
PASSL = True
NT = (((1,), (1,)), ((), ()))
NN = (((1,), (0,)), ((), ()))


def split(value):
    high = value.astype(BF)
    return high, (value - high.astype(F32)).astype(BF)


def dot(a, b, dims):
    return lax.dot_general(a, b, dims, preferred_element_type=F32)


def fold(value):
    rows = value.reshape(32, 8, 256).sum(axis=0)
    return rows[:, :128] + rows[:, 128:]


def kernel(
    gp, own, lr, rr, mo, dir_o, nm_o,
    gv, lv, rv, mv, stx, sty, r1x, r1y, s1x, s1y, r2x, r2y, ez, r1e, s1e, r2e, zt, gbuf, hbuf, lg, rg,
    pt, pr, scx, h32, hb, fin, ob, nm,
    loc, known, es, er, e1s, e1r, e2s, e2r, s1s, s1r, s2s, s2r, zs, zr, ls, lrc, rs, rrc, g1s, g1r, g2s, g2r, ts, tr,
    cxs, cxr, fs, fr,
):
    dp = lax.axis_index("dp")
    shard = lax.axis_index("shard")
    x, y = lax.rem(dp, 4), lax.div(dp, 4)
    z, core = lax.div(shard, 2), lax.rem(shard, 2)
    u = (1 - core) * x + core * y
    v = (1 - core) * y + core * x

    def step(i, k):
        return lax.rem(i + k, 4)

    def to_x(k):
        return {"dp": y * 4 + step(x, k)}

    def to_y(k):
        return {"dp": step(y, k) * 4 + x}

    def to_dp(k):
        return {"dp": step(y, k // 4) * 4 + step(x, k % 4)}

    def to_u(k):
        return {"dp": (1 - core) * (y * 4 + step(x, k)) + core * (step(y, k) * 4 + x)}

    def to_v(k):
        return {"dp": core * (y * 4 + step(x, k)) + (1 - core) * (step(y, k) * 4 + x)}

    def remote(src, dst, ssem, rsem, device):
        return pltpu.make_async_remote_copy(
            src_ref=src, dst_ref=dst, send_sem=ssem, recv_sem=rsem, device_id=device, device_id_type=MESH
        )

    def start_all(copies):
        for copy in copies:
            copy.start()

    def recv_all(copies):
        for copy in copies:
            copy.wait_recv()

    def send_all(copies):
        for copy in copies:
            copy.wait_send()

    load_g = pltpu.make_async_copy(gp.at[0], gv, loc.at[0])
    load_l = pltpu.make_async_copy(lr.at[0], lv, loc.at[1])
    load_r = pltpu.make_async_copy(rr.at[0], rv, loc.at[2])
    load_m = pltpu.make_async_copy(mo.at[0], mv, loc.at[3])
    load_g.start()
    load_r.start()
    load_l.start()
    load_m.start()

    barrier = pltpu.get_barrier_semaphore()
    for k in range(1, 16):
        pl.semaphore_signal(barrier, inc=1, device_id=to_dp(k), device_id_type=MESH)

    def along_z(k):
        return {"shard": lax.rem(z + k + 8, 8) * 2 + core}

    other_core = {"shard": z * 2 + 1 - core}
    cross = ({"shard": lax.rem(z + 1, 8) * 2 + 1 - core}, {"shard": lax.rem(z + 7, 8) * 2 + 1 - core})
    near = (along_z(1), along_z(-1), other_core)
    for device in near + cross:
        pl.semaphore_signal(barrier, inc=1, device_id=device, device_id_type=MESH)

    rounds = (near, (along_z(2), along_z(-2)), (other_core,))

    def tell(i):
        for device in rounds[i]:
            pl.semaphore_signal(known.at[i], inc=1, device_id=device, device_id_type=MESH)

    def hear(i):
        pl.semaphore_wait(known.at[i], len(rounds[i]))

    def block_of(slot):
        found = jnp.int32(0)
        for b in range(16):
            found = jnp.where(own[b] == slot, b, found)
        return found

    def stage(q):
        zq = lax.rem(z + OFFSETS[q], 8)
        for target, staged in enumerate((stx, sty)):
            block = gv[block_of(zq * 2 + target)]
            for i in range(4):
                staged[i, q] = block[16 * i : 16 * i + 16]

    def stage1(c):
        part = pl.ds(*PARTS[c])
        out = []
        for k in range(1, 4):
            out.append(remote(stx.at[step(x, k), part], r1x.at[k - 1, part], s1s.at[k - 1, c, 0], s1r.at[k - 1, c, 0], to_x(k)))
            out.append(remote(sty.at[step(y, k), part], r1y.at[k - 1, part], s1s.at[k - 1, c, 1], s1r.at[k - 1, c, 1], to_y(k)))
        return out

    def sum1(q):
        for staged, got, summed, me in ((stx, r1x, s1x, x), (sty, r1y, s1y, y)):
            total = staged[me, q].astype(F32)
            for k in range(3):
                total = total + got[k, q].astype(F32)
            for j in range(4):
                summed[j, q] = total[:, 256 * j : 256 * j + 256]

    def stage2(c):
        part = pl.ds(*PARTS[c])
        out = []
        for k in range(1, 4):
            out.append(remote(s1x.at[step(y, k), part], r2x.at[k - 1, part], s2s.at[k - 1, c, 0], s2r.at[k - 1, c, 0], to_y(k)))
            out.append(remote(s1y.at[step(x, k), part], r2y.at[k - 1, part], s2s.at[k - 1, c, 1], s2r.at[k - 1, c, 1], to_x(k)))
        return out

    def sum2(q):
        for target, (summed, got, me) in enumerate(((s1x, r2x, y), (s1y, r2y, x))):
            total = summed[me, q]
            for k in range(3):
                total = total + got[k, q]
            zt[target, q, 0], zt[target, q, 1] = split(total)

    def exchange(q, target):
        dst = gbuf.at[shard, y if target == 0 else x]
        device = {"shard": lax.rem(z + OFFSETS[q], 8) * 2 + target}
        return remote(zt.at[target, q], dst, zs.at[target, q], zr.at[q, core], device)

    def send_z(q):
        if OFFSETS[q]:
            exchange(q, 0).start()
            exchange(q, 1).start()
        else:
            @pl.when(core == 0)
            def _():
                exchange(q, 1).start()
                gbuf[shard, y] = zt[0, q]

            @pl.when(core == 1)
            def _():
                exchange(q, 0).start()
                gbuf[shard, x] = zt[1, q]

    def wait_z(q):
        for source in range(2):
            def wait():
                remote(zt.at[0, q], gbuf.at[shard, v], zs.at[0, q], zr.at[q, source], {"shard": shard}).wait_recv()

            if OFFSETS[q]:
                wait()
            else:
                pl.when(core != source)(wait)

    def sent_z(q):
        if OFFSETS[q]:
            exchange(q, 0).wait_send()
            exchange(q, 1).wait_send()
        else:
            pl.when(core == 0)(lambda: exchange(q, 1).wait_send())
            pl.when(core == 1)(lambda: exchange(q, 0).wait_send())

    def early(q, target):
        staged = (stx, sty)[target]
        e = q - EARLY
        device = {"shard": lax.rem(z + OFFSETS[q], 8) * 2 + target}
        return remote(staged.at[:, q], ez.at[:, 2 * e + core], es.at[target, e], er.at[e, core], device)

    def send_early(q):
        if OFFSETS[q]:
            early(q, 0).start()
            early(q, 1).start()
        else:
            @pl.when(core == 0)
            def _():
                early(q, 1).start()
                ez[:, 2 * (q - EARLY)] = stx[:, q]

            @pl.when(core == 1)
            def _():
                early(q, 0).start()
                ez[:, 2 * (q - EARLY) + 1] = sty[:, q]

    def wait_early(q):
        e = q - EARLY
        for source in range(2):
            def wait():
                remote(stx.at[:, q], ez.at[:, 2 * e + source], es.at[0, e], er.at[e, source], {"shard": shard}).wait_recv()

            if OFFSETS[q]:
                wait()
            else:
                pl.when(core != source)(wait)

    def sent_early(q):
        if OFFSETS[q]:
            early(q, 0).wait_send()
            early(q, 1).wait_send()
        else:
            pl.when(core == 0)(lambda: early(q, 1).wait_send())
            pl.when(core == 1)(lambda: early(q, 0).wait_send())

    def early1(q):
        e = q - EARLY
        part = pl.ds(2 * e, 2)
        return [
            remote(ez.at[step(u, k), part], r1e.at[k - 1, part], e1s.at[k - 1, e], e1r.at[k - 1, e], to_u(k))
            for k in range(1, 4)
        ]

    def early2(q):
        e = q - EARLY
        part = pl.ds(2 * e, 2)
        return [
            remote(s1e.at[step(v, k), part], r2e.at[k - 1, part], e2s.at[k - 1, e], e2r.at[k - 1, e], to_v(k))
            for k in range(1, 4)
        ]

    def early_sum1(q):
        for e in (2 * (q - EARLY), 2 * (q - EARLY) + 1):
            total = ez[u, e].astype(F32)
            for k in range(3):
                total = total + r1e[k, e].astype(F32)
            for j in range(4):
                s1e[j, e] = total[:, 256 * j : 256 * j + 256]

    def early_sum2(q):
        for source in range(2):
            e = 2 * (q - EARLY) + source
            total = s1e[v, e]
            for k in range(3):
                total = total + r2e[k, e]
            slot = 2 * lax.rem(z + 8 - OFFSETS[q], 8) + source
            gbuf[slot, v, 0], gbuf[slot, v, 1] = split(total)

    def pair(q):
        return pl.ds(2 * lax.rem(z + 8 - OFFSETS[q], 8), 2)

    class Gather:
        def __init__(self, piece, half, me, to, ssem, rsem, passing):
            own_piece = piece(me)
            self.direct = [
                remote(own_piece, own_piece, ssem.at[0], rsem.at[0], to(1)),
                remote(own_piece, own_piece, ssem.at[1], rsem.at[1], to(3)),
            ]
            if passing:
                after, before = half(step(me, 3), 0), half(step(me, 1), 1)
                self.passed = [
                    remote(after, after, ssem.at[2], rsem.at[2], to(1)),
                    remote(before, before, ssem.at[3], rsem.at[3], to(3)),
                ]
            else:
                self.passed = [remote(own_piece, own_piece, ssem.at[2], rsem.at[2], to(2))]
            self.passing = passing

        def start(self):
            start_all(self.direct)
            if not self.passing:
                start_all(self.passed)

        def go_on(self):
            if self.passing:
                for received, onward in zip(self.direct, self.passed):
                    received.wait_recv()
                    start_all([onward])

        def wait(self):
            if not self.passing:
                recv_all(self.direct)
            recv_all(self.passed)

        def sent(self):
            send_all(self.direct)
            send_all(self.passed)

    def gather1(q):
        return Gather(
            lambda i: gbuf.at[pair(q), i], lambda i, h: gbuf.at[pair(q), i, h], v, to_v, g1s.at[q], g1r.at[q], PASS1[q]
        )

    def gather2(q):
        return Gather(
            lambda i: hbuf.at[:, pair(q), i], lambda i, h: hbuf.at[h, pair(q), i], u, to_u, g2s.at[q], g2r.at[q], PASS2[q]
        )

    def times_right(qs):
        rows = 32 * len(qs)
        total = None
        for j in range(4):
            cols = slice(256 * j, 256 * j + 256)
            high, low = (
                jnp.concatenate([gbuf[pair(i), j, h].reshape(32, 256) for i in qs], axis=0) for h in range(2)
            )
            b_high = rg[:, 0, :, cols].reshape(256, 256)
            b_low = rg[:, 1, :, cols].reshape(256, 256)
            both = dot(jnp.concatenate([high, low], axis=0), b_high, NT)
            part = both[:rows] + both[rows:] + dot(high, b_low, NT)
            total = part if total is None else total + part
        high, low = split(total)
        for i, q in enumerate(qs):
            hbuf[0, pair(q), u] = high[32 * i : 32 * i + 32].reshape(2, 16, 256)
            hbuf[1, pair(q), u] = low[32 * i : 32 * i + 32].reshape(2, 16, 256)

    def left_times(part):
        high, low = [], []
        for q in part:
            cols = pl.ds(pl.multiple_of(128 * lax.rem(z + 8 - OFFSETS[q], 8), 128), 128)
            high.append(lg[:, 0, :, cols].reshape(256, 128))
            low.append(lg[:, 1, :, cols].reshape(256, 128))
        a_high, a_low = (jnp.concatenate(cols, axis=1) for cols in (high, low))
        b_high, b_low = (
            jnp.concatenate([hbuf[h, pair(q)].reshape(128, 256) for q in part], axis=0) for h in range(2)
        )
        return dot(a_high, b_high, NN) + dot(a_high, b_low, NN) + dot(a_low, b_high, NN)

    rights = Gather(lambda i: rg.at[i], lambda i, h: rg.at[i, h], u, to_u, rs, rrc, PASSR)
    lefts = Gather(lambda i: lg.at[i], lambda i, h: lg.at[i, h], v, to_v, ls, lrc, PASSL)

    def slots(c):
        return range(PARTS[c][0], PARTS[c][0] + PARTS[c][1])

    load_g.wait()
    for c in range(CHUNKS):
        for q in slots(c):
            stage(q)
        if c == 0:
            pl.semaphore_wait(barrier, 20)
        start_all(stage1(c))
        if c == 0:
            tell(0)
            for q in slots(CHUNKS):
                stage(q)
                send_early(q)

    load_r.wait()
    rg[u, 0], rg[u, 1] = split(rv[...])
    load_l.wait()
    lg[v, 0], lg[v, 1] = split(lv[...])

    def sum_first(c):
        recv_all(stage1(c))
        for q in slots(c):
            sum1(q)
        start_all(stage2(c))

    def sum_second(c):
        recv_all(stage2(c))
        for q in slots(c):
            sum2(q)
            send_z(q)

    def spread_rows(c):
        for q in slots(c):
            if c < CHUNKS:
                wait_z(q)
            else:
                recv_all(early2(q))
                early_sum2(q)
            gather1(q).start()

    def early_first():
        for q in slots(CHUNKS):
            wait_early(q)
            start_all(early1(q))

    def early_second():
        for q in slots(CHUNKS):
            recv_all(early1(q))
            early_sum1(q)
            start_all(early2(q))

    def pass_rows(c):
        for q in slots(c):
            gather1(q).go_on()

    def multiply_right(c):
        for q in slots(c):
            gather1(q).wait()
        times_right(slots(c))
        for q in slots(c):
            gather2(q).start()

    def pass_products(c):
        for q in slots(c):
            gather2(q).go_on()

    def multiply_left(c):
        for q in slots(c):
            gather2(q).wait()
        product = left_times(slots(c)).reshape(4, 64, 256)
        pt[...] = product if c == 0 else pt[...] + product

    def norms(kind):
        part = scx.at[kind, dp]
        return [
            remote(part, part, cxs.at[kind, k], cxr.at[kind, k], to_dp(k))
            for k in (10, 6, 14, 9, 11, 5, 7, 13, 15, 2, 8, 1, 3, 4, 12)
        ]

    def norm_of_gradient():
        tile = gbuf[:, v]
        tile = (tile[:, 0].astype(F32) + tile[:, 1].astype(F32)).reshape(256, 256)
        scx[0, dp] = fold(tile * tile)
        start_all(norms(0))

    sum_first(0)
    hear(0)
    tell(1)
    early_first()
    hear(1)
    tell(2)
    sum_first(1)
    sum_first(2)
    hear(2)
    rights.start()
    sum_second(0)
    sum_second(2)
    sum_second(1)
    early_second()
    rights.go_on()
    lefts.start()
    spread_rows(0)
    spread_rows(1)
    spread_rows(2)
    spread_rows(3)
    pass_rows(0)
    pass_rows(1)
    pass_rows(2)
    pass_rows(3)
    norm_of_gradient()
    lefts.go_on()
    rights.wait()
    multiply_right(0)
    multiply_right(1)
    multiply_right(2)
    multiply_right(3)
    pass_products(0)
    pass_products(1)
    pass_products(2)
    lefts.wait()
    multiply_left(0)
    pass_products(3)
    multiply_left(1)
    multiply_left(3)
    multiply_left(2)

    tile = pt[...].reshape(256, 256)
    scx[1, dp] = fold(tile * tile)

    turn = [remote(pt.at[step(v, k)], pr.at[v], ts.at[k - 1], tr.at[k - 1], to_v(k)) for k in range(1, 4)]
    start_all(norms(1))
    start_all(turn)
    pr[v] = pt[v]
    load_m.wait()
    for c in range(CHUNKS):
        send_all(stage1(c))
    for c in range(CHUNKS):
        send_all(stage2(c))
    for q in range(EARLY):
        sent_z(q)
    for q in slots(CHUNKS):
        sent_early(q)
        send_all(early1(q))
        send_all(early2(q))
    recv_all(turn)
    recv_all(norms(0))
    recv_all(norms(1))
    entries = 1024 * 1024
    grad_total = jnp.sum(scx[0].sum(axis=0), keepdims=True)
    prec_total = jnp.sum(scx[1].sum(axis=0), keepdims=True)
    scale = jnp.sqrt(grad_total / entries + epsilon) / jnp.sqrt(prec_total / entries + epsilon)

    def update(columns):
        for j in range(8):
            cols = slice(128 * j, 128 * j + 128)
            graft = columns(j) * scale
            moved = decay_rate * mv[:, cols] + graft
            nm_o[0, :, cols] = moved
            h32[:, cols] = decay_rate * moved + graft

    @pl.when(core == 0)
    def _():
        update(lambda j: pr[j // 2, :, 128 * (j % 2) : 128 * (j % 2) + 128])

    @pl.when(core == 1)
    def _():
        def columns(j):
            strip = slice(64 * (j // 2), 64 * (j // 2) + 64)
            first = 2 * (j % 2)
            return jnp.concatenate([pr[first, :, strip], pr[first + 1, :, strip]], axis=1)

        update(columns)

    hb[...] = h32[...].reshape(16, 4, 1024).astype(BF)

    def back(k):
        to = lax.rem(shard + k, 16)
        return remote(hb.at[to], fin.at[shard], fs.at[k], fr.at[k], {"shard": to})

    order = (8, 9, 7, 10, 6, 11, 5, 12, 4, 13, 3, 14, 2, 15, 1)
    for k in order:
        back(k).start()
    fin[shard] = hb[shard]
    send_all(norms(0))
    send_all(norms(1))
    send_all(turn)
    rights.sent()
    lefts.sent()
    for q in range(8):
        gather1(q).sent()
        gather2(q).sent()
    for k in order:
        back(k).wait_recv()
    for b in range(16):
        dir_o[b] = fin[own[b]]
    for k in order:
        back(k).wait_send()


def last(d_in, m_in, d_out, m_out, sem):
    copies = [pltpu.make_async_copy(m_in, m_out, sem.at[0]), pltpu.make_async_copy(d_in, d_out, sem.at[1])]
    for copy in copies:
        copy.start()
    for copy in copies:
        copy.wait()


def body(grad_partial, owner_slots, left_roots, right_roots, momentum):
    dma = pltpu.SemaphoreType.DMA
    any_space = pl.BlockSpec(memory_space=pl.ANY)
    direction, new_momentum = pl.pallas_call(
        kernel,
        out_shape=(
            jax.ShapeDtypeStruct((16, 4, 1024), BF),
            jax.ShapeDtypeStruct((1, 64, 1024), F32),
        ),
        in_specs=[any_space, pl.BlockSpec(memory_space=pltpu.SMEM), any_space, any_space, any_space],
        out_specs=(pl.BlockSpec(memory_space=pltpu.VMEM),) * 2,
        scratch_shapes=[
            pltpu.VMEM((16, 64, 1024), BF),
            pltpu.VMEM((64, 1024), F32),
            pltpu.VMEM((64, 1024), F32),
            pltpu.VMEM((64, 1024), F32),
            pltpu.VMEM((4, 8, 16, 1024), BF),
            pltpu.VMEM((4, 8, 16, 1024), BF),
            pltpu.VMEM((3, 8, 16, 1024), BF),
            pltpu.VMEM((3, 8, 16, 1024), BF),
            pltpu.VMEM((4, 8, 16, 256), F32),
            pltpu.VMEM((4, 8, 16, 256), F32),
            pltpu.VMEM((3, 8, 16, 256), F32),
            pltpu.VMEM((3, 8, 16, 256), F32),
            pltpu.VMEM((4, 6, 16, 1024), BF),
            pltpu.VMEM((3, 6, 16, 1024), BF),
            pltpu.VMEM((4, 6, 16, 256), F32),
            pltpu.VMEM((3, 6, 16, 256), F32),
            pltpu.VMEM((2, 8, 2, 16, 256), BF),
            pltpu.VMEM((16, 4, 2, 16, 256), BF),
            pltpu.VMEM((2, 16, 4, 16, 256), BF),
            pltpu.VMEM((4, 2, 64, 1024), BF),
            pltpu.VMEM((4, 2, 64, 1024), BF),
            pltpu.VMEM((4, 64, 256), F32),
            pltpu.VMEM((4, 64, 256), F32),
            pltpu.VMEM((2, 16, 8, 128), F32),
            pltpu.VMEM((64, 1024), F32),
            pltpu.VMEM((16, 4, 1024), BF),
            pltpu.VMEM((16, 4, 1024), BF),
            pltpu.VMEM((16, 4, 1024), BF),
            pltpu.VMEM((64, 1024), F32),
            dma((6,)),
            pltpu.SemaphoreType.REGULAR((3,)),
            dma((2, 3)), dma((3, 2)),
            dma((3, 3)), dma((3, 3)), dma((3, 3)), dma((3, 3)),
            dma((3, CHUNKS, 2)), dma((3, CHUNKS, 2)),
            dma((3, CHUNKS, 2)), dma((3, CHUNKS, 2)),
            dma((2, 8)), dma((8, 2)),
            dma((4,)), dma((4,)), dma((4,)), dma((4,)),
            dma((8, 4)), dma((8, 4)), dma((8, 4)), dma((8, 4)),
            dma((3,)), dma((3,)),
            dma((2, 16)), dma((2, 16)),
            dma((16,)), dma((16,)),
        ],
        compiler_params=pltpu.CompilerParams(
            collective_id=0, has_side_effects=True, vmem_limit_bytes=54800 * 1024
        ),
    )(grad_partial, owner_slots, jnp.swapaxes(left_roots, 1, 2), right_roots, momentum)
    vmem = pl.BlockSpec(memory_space=pltpu.VMEM)
    return pl.pallas_call(
        last,
        out_shape=(
            jax.ShapeDtypeStruct((16, 4, 1024), BF),
            jax.ShapeDtypeStruct((1, 64, 1024), F32),
        ),
        in_specs=[vmem, vmem],
        out_specs=(any_space, any_space),
        scratch_shapes=[dma((2,))],
        compiler_params=pltpu.CompilerParams(vmem_limit_bytes=2 * 2**20),
    )(direction, new_momentum)


def solution(mesh):
    return jax.shard_map(
        body,
        mesh=mesh,
        in_specs=(
            P("dp", None, "shard", None),
            P(),
            P("shard", None, "dp"),
            P("shard", "dp", None),
            P("shard", "dp", None),
        ),
        out_specs=(P(None, ("dp", "shard"), None), P("shard", "dp", None)),
        check_vma=False,
    )
```
